32 devices in a mesh: aux: 8 (over z, y), orb: 4 (over x, core).
Axes of the slice: x: 2, y: 2, z: 4, core: 2. Of those that a mesh axis runs over, the one named last changes fastest.
Arguments:
- three_index: bfloat16 [64, 1600, 1600], P('aux', 'orb'), may hold values from -40 to 40, as said below
- density: bfloat16 [64, 1600, 160], P('aux', 'orb'), may hold values from -0.01953125 to 0.01953125
- hess_diag: float32 [1440, 160], replicated, may hold values from 0.5 to 4
Outputs:
- ov_new: bfloat16 [4, 64, 57600], P('orb', None, 'aux')
The draws below stay inside these ranges and needn't reach their ends.
Inputs may be any that keep to these rules, and one draw needn't show every extreme that they name: three_index[q, p, r] equals three_index[q, r, p].
All inputs are finite; a program needn't handle non-finite values.
Results may differ from the reference program's by a relative error of at most 0.0065.
Values may be sent and summed in bfloat16 or wider, within the bound.
No kernel may reach another device: no remote copies, remote signals or barrier semaphores. Data moves between devices by JAX's collectives and lax.ppermute only.
A program may use at most 64 MiB of HBM per device.

```python
import math
import jax
import jax.numpy as jnp
from jax import lax

NO = 160
NV = 1440
NMO = 1600
NAUX = 64
OBLK = 40
N_ORB = 4


def draw_three_index(key, part):
    key = jax.random.fold_in(key, 7)

    def one_slice(index):
        sub_key = jax.random.fold_in(key, index + 2)
        raw_draw = jax.random.normal(sub_key, (NMO, NMO), jnp.float32)
        symmetric = (raw_draw + raw_draw.T) * 0.7071
        return symmetric.astype(jnp.bfloat16)
    return lax.map(one_slice, jnp.arange(NAUX, dtype=jnp.int32))


def levels(rng, shape, pieces, least, top_value):
    gain = 1.0
    for axis_at, blocks in pieces:
        steps = jax.random.uniform(jax.random.fold_in(jax.random.fold_in(rng, 6), axis_at), (blocks,), jnp.float32, least / len(pieces), top_value / len(pieces))
        gain = gain * jnp.repeat(jnp.exp(steps), shape[axis_at] // blocks).reshape((-1,) + (1,) * (len(shape) - 1 - axis_at))
    return gain


def noise(own_key, extent, spread, limit, shards=(), kind=jnp.bfloat16):
    entries = spread * jax.random.normal(own_key, extent, jnp.float32)
    if shards:
        entries = entries * levels(own_key, extent, shards, -0.22, 0.18)
    return jnp.clip(entries, -limit, limit).astype(kind)


def setup_inputs(seed: int = 0) -> dict:
    arg_keys = jax.random.split(jax.random.key(seed), 4)
    return {
        "three_index": draw_three_index(jax.random.fold_in(arg_keys[3], 71), 0),
        "density": noise(arg_keys[1], (NAUX, NMO, NO), (NAUX * NMO) ** -0.5, 0.01953125, ((0, 8), (1, 4))),
        "hess_diag": jnp.clip(jnp.exp(jax.random.uniform(arg_keys[2], (NV, NO), jnp.float32, math.log(0.5), math.log(4.0))), 0.5, 4.0),
    }


def reference(three_index, density, hess_diag):
    highest = lax.Precision.HIGHEST

    def add_fock(total, pair):
        b_slice, d_slice = pair
        return (total + jnp.dot(b_slice.T, d_slice, preferred_element_type=jnp.float32), None)
    fock_full, _ = lax.scan(add_fock, jnp.zeros((NMO, NO), jnp.float32), (three_index, density))
    fock_vo = fock_full[NO:]
    generator = -fock_vo / hess_diag
    gen_norm = jnp.sqrt(jnp.sum(generator * generator))
    rotation = generator * jnp.minimum(1.0, math.sqrt(NO) / gen_norm)
    kmat = jnp.zeros((NMO, NMO), jnp.float32)
    kmat = kmat.at[NO:, :NO].set(rotation)
    kmat = kmat.at[:NO, NO:].set(-rotation.T)
    ident = jnp.eye(NMO, dtype=jnp.float32)
    power = ident
    unitary = ident
    for order in range(1, 5):
        power = jnp.dot(power, kmat, precision=highest) / float(order)
        unitary = unitary + power
    unitary_b = unitary.astype(jnp.bfloat16)
    occ_cols = unitary_b[:, :NO]
    vir_cols = unitary_b[:, NO:]

    def rotate_one(b_slice):
        half_rot = jnp.dot(b_slice, occ_cols, preferred_element_type=jnp.float32).astype(jnp.bfloat16)
        return jnp.dot(half_rot.T, vir_cols, preferred_element_type=jnp.float32).astype(jnp.bfloat16)
    rotated = lax.map(rotate_one, three_index)
    return jnp.transpose(rotated.reshape(NAUX, N_ORB, OBLK * NV), (1, 0, 2))
```

```python
import functools
import math

import jax
import jax.numpy as jnp
import numpy as np
from jax import lax
from jax.experimental import pallas as pl
from jax.experimental.pallas import tpu as pltpu
from jax.sharding import PartitionSpec as P

BOTH = ("aux", "orb")
F32 = jnp.float32
BF16 = jnp.bfloat16
LANES = 128
MIB = 1 << 20


def matmul(a, b, dims):
    return lax.dot_general(a, b, (dims, ((), ())), preferred_element_type=F32)


NN = ((1,), (0,))
NT = ((1,), (1,))
TN = ((0,), (0,))


def my_index(n_orb):
    return lax.axis_index("aux") * n_orb + lax.axis_index("orb")


def swap(x, masks):
    return lax.ppermute(x, BOTH, [(d, d ^ mask) for d, mask in enumerate(masks)])


def tracks_of(n_dev):
    bits = n_dev.bit_length() - 1
    return [1, 2, *range(3, bits)], [2, 1, *range(bits - 1, 2, -1)]


def bit(index, which):
    return (index // (1 << which)) % 2


def half_of(index, n_dev):
    return sum(bit(index, k) for k in range(n_dev.bit_length() - 1)) % 2


def assemble(sources, width, rows):
    lane = lax.broadcasted_iota(jnp.int32, (rows, LANES), 1)
    rolled = {}

    def source_tile(which, tile, turn):
        key = (which, tile, turn)
        if key not in rolled:
            value = sources[which][0](tile)
            rolled[key] = pltpu.roll(value, turn, 1) if turn else value
        return rolled[key]

    tiles = []
    for start in range(0, width, LANES):
        result, end_done = None, 0
        for which, (_, src, dst, count) in enumerate(sources):
            low, high = max(dst, start), min(dst + count, start + LANES)
            turn = (dst - src) % LANES
            at = low
            while at < high:
                from_lane = at - dst + src
                tile = from_lane // LANES
                stop = min(high, at + LANES - from_lane % LANES)
                value = source_tile(which, tile, turn)
                if result is None:
                    result = value
                    if at > start:
                        result = jnp.where(lane >= at - start, value, 0.0)
                else:
                    result = jnp.where(lane >= at - start, value, result)
                end_done = stop - start
                at = stop
        if end_done < LANES:
            result = jnp.where(lane < end_done, result, 0.0)
        tiles.append(result)
    return tiles


def fock_kernel(n_orb, n_dev, splits, three_hbm, dens_ref, keep_ref, send_ref, three_ref, acc_ref, sems):
    n_tiles = acc_ref.shape[0]
    q_loc, _, n_mo = three_ref.shape
    n_occ = dens_ref.shape[1]
    base = n_occ // LANES * LANES
    copies = []
    for q in range(q_loc):
        copies.append(pltpu.make_async_copy(three_hbm.at[q], three_ref.at[q], sems.at[q]))
        copies[q].start()
    for q in range(q_loc):
        copies[q].wait()
        part = matmul(dens_ref[q], three_ref[q, :, base:], NN)
        for t in range(n_tiles):
            stop = min(LANES, n_mo - base - t * LANES)
            piece = part[:, t * LANES : t * LANES + stop]
            if q:
                acc_ref[t, :, :stop] += piece
            else:
                if stop < LANES:
                    acc_ref[t] = jnp.zeros(acc_ref.shape[1:], F32)
                acc_ref[t, :, :stop] = piece
    me = my_index(n_orb)
    mine = half_of(me, n_dev)
    half, quarter = n_tiles // 2, n_tiles // 4
    for ref, side in ((keep_ref, mine), (send_ref, 1 - mine)):
        lead = jnp.where(side == 0, bit(me, splits[0]), bit(me, splits[1]))
        for j in range(half):
            first = jnp.where(lead == j // quarter, 0, quarter)
            ref[j] = acc_ref[side * half + first + j % quarter].astype(ref.dtype)


def rotation_kernel(n_orb, n_dev, splits, mine_ref, other_ref, hess_ref, sel_ref, chosen_ref, left_ref, rot_ref, fock_ref, u_ref):
    n_occ, width = fock_ref.shape
    half = mine_ref.shape[0]
    quarter = half // 2
    base = n_occ // LANES * LANES
    n_mo = chosen_ref.shape[1]
    me = my_index(n_orb)
    mine = half_of(me, n_dev)
    for t in range(2 * half):
        side = t // half
        first = jnp.where(bit(me, splits[side]) == t % half // quarter, 0, quarter)
        at = first + t % quarter
        fock_ref[:, t * LANES : (t + 1) * LANES] = jnp.where(
            mine == side, mine_ref[at].astype(F32), other_ref[at].astype(F32))
    gen = -fock_ref[...] / hess_ref[...]
    square = jnp.sum(jnp.sum(gen * gen, axis=0, keepdims=True), axis=1, keepdims=True)
    rot = gen * jnp.minimum(1.0, math.sqrt(n_occ) / jnp.sqrt(square))
    rot_b = rot.astype(BF16)
    rot_ref[...] = rot_b
    over = matmul(rot_b, rot_b, NT)
    over_b = over.astype(BF16)
    over2 = matmul(over_b, over_b, NN)
    over_rot = matmul(over_b, rot_b, NN)
    eye = jnp.where(
        lax.broadcasted_iota(jnp.int32, (n_occ, n_occ), 0) == lax.broadcasted_iota(jnp.int32, (n_occ, n_occ), 1),
        1.0, 0.0)
    u_oo = (eye - over / 2.0 + over2 / 24.0).astype(BF16)
    u_ref[:, :base] = u_oo[:, :base]
    u_ref[:, base:] = (rot - over_rot / 6.0).astype(BF16)
    u_ref[:, base:n_occ] = u_oo[:, base:]
    l_oo = (over / 6.0 - eye).astype(BF16)
    left_ref[:, :base] = l_oo[:, :base]
    left_ref[:, base:] = (over_rot / 24.0 - rot / 2.0).astype(BF16)
    left_ref[:, base:n_occ] = l_oo[:, base:]
    chosen_ref[...] = matmul(sel_ref[...], u_ref[:, :n_mo], NN).astype(BF16)


def half_kernel(n_rows, main, chosen_ref, three_ref, sent_ref, rem_ref, half_ref):
    q_loc, r_loc, n_mo = three_ref.shape
    rem = r_loc - main
    n_dev, dest_rows = sent_ref.shape[:2]

    def store(value, row):
        for k in range(n_rows):
            half_ref[pl.ds(row(k), n_dev, stride=dest_rows), :] = value[k * n_dev : (k + 1) * n_dev, :]

    chosen = chosen_ref[...]
    for q in range(q_loc):
        product = matmul(chosen, three_ref[q, :main, :], NT)
        for c in range(main // LANES):
            store(product[:, c * LANES : (c + 1) * LANES], lambda k, c=c, q=q: (c * n_rows + k) * q_loc + q)
        rem_ref[q * rem : (q + 1) * rem, :] = three_ref[q, main:, :]
    store(matmul(chosen, rem_ref[...], NT), lambda k: main // LANES * n_rows * q_loc + k)
    for d in range(n_dev):
        sent_ref[d] = half_ref[d * dest_rows : (d + 1) * dest_rows, :].astype(BF16)


def owner_kernel(n_rows, n_aux, q_loc, r_loc, main, got_ref, left_ref, rot_ref, out_ref):
    n_orb = got_ref.shape[1]
    places = pl.ds(pl.program_id(0) * n_aux, n_aux)
    n_occ, wide = left_ref.shape
    width = rot_ref.shape[1]
    base = wide - width
    n_mo = n_orb * r_loc
    n_vir = n_mo - n_occ
    rem = r_loc - main
    group = n_rows * q_loc
    rows = n_aux * group
    lane_q = lax.broadcasted_iota(jnp.int32, (n_aux, q_loc, LANES), 2) // rem
    own_q = lane_q == lax.broadcasted_iota(jnp.int32, (n_aux, q_loc, LANES), 1)
    e_row = lax.broadcasted_iota(jnp.int32, (LANES, LANES), 0) % rem
    e_col = lax.broadcasted_iota(jnp.int32, (LANES, LANES), 1)

    sources = []
    rest = jnp.zeros((rows, LANES), F32)
    for b in range(n_orb):
        block = got_ref[places, b, :, :].astype(F32)
        pieces = [block[:, c * group : (c + 1) * group, :].reshape(rows, LANES) for c in range(main // LANES)]
        last = main // LANES * group
        spread = [
            jnp.where(own_q, jnp.broadcast_to(block[:, last + k : last + k + 1, :], own_q.shape), 0.0)
            for k in range(n_rows)
        ]
        spread = jnp.concatenate(spread, 1).reshape(rows, LANES).astype(BF16)
        rest = rest + matmul(spread, jnp.where(e_row + b * rem == e_col, 1.0, 0.0).astype(BF16), NN)
        sources.append((lambda tile, pieces=pieces: pieces[tile], 0, b * r_loc, main))
    for b in range(n_orb):
        sources.append((lambda tile: rest, b * rem, b * r_loc + main, rem))
    sources.sort(key=lambda entry: entry[2])
    half = jnp.concatenate(assemble(sources, wide, rows), 1)
    inner = matmul(half.astype(BF16), left_ref[...], NT).astype(BF16)
    total = half[:, base:] + matmul(inner, rot_ref[...], NN)
    total = total.reshape(n_aux, group, width)
    per_row = [total[:, k * q_loc : (k + 1) * q_loc, :].reshape(n_aux * q_loc, width) for k in range(n_rows)]
    sources = [
        (lambda tile, value=value: value[:, tile * LANES : (tile + 1) * LANES], n_occ - base, k * n_vir, n_vir)
        for k, value in enumerate(per_row)
    ]
    length = n_rows * n_vir
    for at, value in enumerate(assemble(sources, length, n_aux * q_loc)):
        stop = min(length, (at + 1) * LANES)
        out_ref[:, at * LANES : stop] = value[:, : stop - at * LANES].astype(BF16)


def on_device(n_aux, n_orb, three_index, density, hess_diag):
    n_dev = n_aux * n_orb
    q_loc, r_loc, n_mo = three_index.shape
    n_occ = density.shape[2]
    n_vir = n_mo - n_occ
    occ_blk = n_occ // n_orb
    pairs = occ_blk * n_vir // n_aux
    base = n_occ // LANES * LANES
    tiles = -(-(n_mo - base) // LANES)
    width = tiles * LANES
    main = r_loc // LANES * LANES
    assert n_dev & (n_dev - 1) == 0 and n_dev >= 8 and tiles % 4 == 0
    tracks = tracks_of(n_dev)
    splits = (tracks[0][0], tracks[1][0])
    whole = lambda *shape: pl.BlockSpec(shape, lambda *_: (0,) * len(shape))
    in_vmem = pl.BlockSpec(memory_space=pltpu.VMEM)

    half_shape = (tiles // 2, n_occ, LANES)
    in_hbm = pl.BlockSpec(memory_space=pltpu.HBM)
    keep, send, three_vmem = pl.pallas_call(
        functools.partial(fock_kernel, n_orb, n_dev, splits),
        in_specs=[in_hbm, in_vmem],
        out_specs=[in_vmem] * 3,
        out_shape=[
            jax.ShapeDtypeStruct(half_shape, F32),
            jax.ShapeDtypeStruct(half_shape, BF16),
            jax.ShapeDtypeStruct(three_index.shape, BF16),
        ],
        scratch_shapes=[
            pltpu.VMEM((tiles, n_occ, LANES), F32),
            pltpu.SemaphoreType.DMA((q_loc,)),
        ],
        compiler_params=pltpu.CompilerParams(vmem_limit_bytes=38 * MIB),
        cost_estimate=pl.CostEstimate(
            flops=2 * q_loc * r_loc * n_occ * n_mo, bytes_accessed=2 * q_loc * r_loc * n_mo, transcendentals=0),
        name="fock",
    )(three_index, density.transpose(0, 2, 1))
    hess = jnp.pad(
        hess_diag.T, ((0, 0), (n_occ - base, width - (n_mo - base))), constant_values=jnp.inf)

    masks = [[1 | 1 << tracks[half_of(d, n_dev)][k] for d in range(n_dev)] for k in range(len(tracks[0]))]
    part = keep + swap(send, [1] * n_dev).astype(F32)
    part = part[: tiles // 4] + swap(part[tiles // 4 :].astype(BF16), masks[0]).astype(F32)
    for mask in masks[1:]:
        part = part + swap(part.astype(BF16), mask).astype(F32)
    part = part.astype(BF16)
    held = jnp.concatenate([part, swap(part, masks[0])], 0)
    other = swap(held, [1] * n_dev)

    first = [p * pairs // n_vir for p in range(n_aux)]
    n_rows = max(-(-(p + 1) * pairs // n_vir) - first[p] for p in range(n_aux))
    sel = np.zeros((n_rows, n_aux, n_orb, n_occ), np.float32)
    for k in range(n_rows):
        for p in range(n_aux):
            for b in range(n_orb):
                sel[k, p, b, b * occ_blk + min(first[p] + k, occ_blk - 1)] = 1.0
    sel = jnp.asarray(sel.reshape(n_rows * n_dev, n_occ), BF16)

    dest_rows = -(-(main // LANES * n_rows * q_loc + n_rows) // 16) * 16
    wide = base + width
    chosen, left, rot = pl.pallas_call(
        functools.partial(rotation_kernel, n_orb, n_dev, splits),
        in_specs=[in_vmem] * 4,
        out_specs=[in_vmem] * 3,
        out_shape=[
            jax.ShapeDtypeStruct((n_rows * n_dev, n_mo), BF16),
            jax.ShapeDtypeStruct((n_occ, wide), BF16),
            jax.ShapeDtypeStruct((n_occ, width), BF16),
        ],
        scratch_shapes=[pltpu.VMEM((n_occ, width), F32), pltpu.VMEM((n_occ, wide), BF16)],
        compiler_params=pltpu.CompilerParams(vmem_limit_bytes=16 * MIB),
        cost_estimate=pl.CostEstimate(flops=8 * n_occ * n_occ * n_mo, bytes_accessed=4 * MIB, transcendentals=0),
        name="rotation",
    )(held, other, hess, sel)
    sent = pl.pallas_call(
        functools.partial(half_kernel, n_rows, main),
        in_specs=[in_vmem] * 2,
        out_specs=in_vmem,
        out_shape=jax.ShapeDtypeStruct((n_dev, dest_rows, LANES), BF16),
        scratch_shapes=[
            pltpu.VMEM((q_loc * (r_loc - main), n_mo), BF16),
            pltpu.VMEM((n_dev * dest_rows, LANES), F32),
        ],
        compiler_params=pltpu.CompilerParams(vmem_limit_bytes=40 * MIB),
        cost_estimate=pl.CostEstimate(
            flops=2 * q_loc * r_loc * n_rows * n_dev * n_mo, bytes_accessed=2 * q_loc * r_loc * n_mo, transcendentals=0),
        name="half_rotation",
    )(chosen, three_vmem)

    got = lax.all_to_all(sent, BOTH, 0, 0, tiled=True).reshape(n_aux, n_orb, dest_rows, LANES)
    aux_step = min(n_aux, 8)
    out = pl.pallas_call(
        functools.partial(owner_kernel, n_rows, aux_step, q_loc, r_loc, main),
        grid=(n_aux // aux_step,),
        in_specs=[in_vmem] * 3,
        out_specs=pl.BlockSpec((aux_step * q_loc, n_rows * n_vir), lambda g: (g, 0)),
        out_shape=jax.ShapeDtypeStruct((n_aux * q_loc, n_rows * n_vir), BF16),
        compiler_params=pltpu.CompilerParams(vmem_limit_bytes=40 * MIB),
        cost_estimate=pl.CostEstimate(
            flops=4 * n_aux * q_loc * n_rows * n_occ * n_mo, bytes_accessed=8 * MIB, transcendentals=0),
        name="owner_rows",
    )(got, left, rot)
    if n_rows * n_vir != pairs:
        start = (lax.axis_index("aux") * pairs) % n_vir
        out = lax.dynamic_slice_in_dim(out, start, pairs, 1)
    return out[None]


def solution(mesh):
    def body(*args):
        return on_device(mesh.shape["aux"], mesh.shape["orb"], *args)

    return jax.shard_map(
        body,
        mesh=mesh,
        in_specs=(P("aux", "orb", None), P("aux", "orb", None), P()),
        out_specs=P("orb", None, "aux"),
        check_vma=False,
    )
```

```python
import functools
import math

import jax
import jax.numpy as jnp
import numpy as np
from jax import lax
from jax.experimental import pallas as pl
from jax.experimental.pallas import tpu as pltpu
from jax.sharding import PartitionSpec as P

BOTH = ("aux", "orb")
F32 = jnp.float32
BF16 = jnp.bfloat16
LANES = 128
MIB = 1 << 20


def matmul(a, b, dims):
    return lax.dot_general(a, b, (dims, ((), ())), preferred_element_type=F32)


NN = ((1,), (0,))
NT = ((1,), (1,))
TN = ((0,), (0,))


def my_index(n_orb):
    return lax.axis_index("aux") * n_orb + lax.axis_index("orb")


def swap(x, masks):
    return lax.ppermute(x, BOTH, [(d, d ^ mask) for d, mask in enumerate(masks)])


def tracks_of(n_dev):
    bits = n_dev.bit_length() - 1
    return [1, 2, *range(3, bits)], [2, 1, *range(bits - 1, 2, -1)]


def bit(index, which):
    return (index // (1 << which)) % 2


def half_of(index, n_dev):
    return sum(bit(index, k) for k in range(n_dev.bit_length() - 1)) % 2


def assemble(sources, width, rows):
    lane = lax.broadcasted_iota(jnp.int32, (rows, LANES), 1)
    rolled = {}

    def source_tile(which, tile, turn):
        key = (which, tile, turn)
        if key not in rolled:
            value = sources[which][0](tile)
            rolled[key] = pltpu.roll(value, turn, 1) if turn else value
        return rolled[key]

    tiles = []
    for start in range(0, width, LANES):
        result, end_done = None, 0
        for which, (_, src, dst, count) in enumerate(sources):
            low, high = max(dst, start), min(dst + count, start + LANES)
            turn = (dst - src) % LANES
            at = low
            while at < high:
                from_lane = at - dst + src
                tile = from_lane // LANES
                stop = min(high, at + LANES - from_lane % LANES)
                value = source_tile(which, tile, turn)
                if result is None:
                    result = value
                    if at > start:
                        result = jnp.where(lane >= at - start, value, 0.0)
                else:
                    result = jnp.where(lane >= at - start, value, result)
                end_done = stop - start
                at = stop
        if end_done < LANES:
            result = jnp.where(lane < end_done, result, 0.0)
        tiles.append(result)
    return tiles


def fock_kernel(n_orb, n_dev, tracks, three_hbm, dens_ref, *refs):
    *part_refs, three_ref, acc_ref, sems = refs
    q_loc, _, n_mo = three_ref.shape
    n_occ = dens_ref.shape[1]
    n_tiles = acc_ref.shape[0] // n_occ
    base = n_occ // LANES * LANES
    copies = []
    for q in range(q_loc):
        copies.append(pltpu.make_async_copy(three_hbm.at[q], three_ref.at[q], sems.at[q]))
        copies[q].start()
    for q in range(q_loc):
        copies[q].wait()
        part = matmul(dens_ref[q], three_ref[q, :, base:], NN)
        for t in range(n_tiles):
            stop = min(LANES, n_mo - base - t * LANES)
            rows = slice(t * n_occ, (t + 1) * n_occ)
            piece = part[:, t * LANES : t * LANES + stop]
            if q:
                acc_ref[rows, :stop] += piece
            else:
                if stop < LANES:
                    acc_ref[rows, :] = jnp.zeros((n_occ, LANES), F32)
                acc_ref[rows, :stop] = piece
    me = my_index(n_orb)
    mine = half_of(me, n_dev)
    n_rows = n_tiles * n_occ // 8
    for chain in (0, 1):
        for ref, side in zip(part_refs[chain::2], (mine, 1 - mine)):
            lead = jnp.where(side == 0, bit(me, tracks[0][0]), bit(me, tracks[1][0]))
            for j in (0, 1):
                start = pl.multiple_of((side * 4 + chain * 2 + (lead + j) % 2) * n_rows, n_rows)
                ref[j] = acc_ref[pl.ds(start, n_rows), :].astype(ref.dtype)


def rotation_kernel(n_orb, n_dev, tracks, mine_0, mine_1, other_0, other_1, hess_ref, sel_ref, chosen_ref, left_ref, rot_ref, fock_ref, u_ref):
    n_occ, width = fock_ref.shape
    base = n_occ // LANES * LANES
    n_mo = chosen_ref.shape[0]
    mine_refs, other_refs = (mine_0, mine_1), (other_0, other_1)
    n_rows = mine_0.shape[1]
    step = math.gcd(n_rows, n_occ)
    me = my_index(n_orb)
    mine = half_of(me, n_dev)
    for start in range(0, 8 * n_rows, step):
        tile, row = divmod(start, n_occ)
        piece, at = divmod(start, n_rows)
        side, chain, j = piece // 4, piece // 2 % 2, piece % 2
        place = (j + bit(me, tracks[side][0])) % 2
        rows = slice(at, at + step)
        fock_ref[row : row + step, tile * LANES : (tile + 1) * LANES] = jnp.where(
            mine == side, mine_refs[chain][place, rows, :].astype(F32), other_refs[chain][place, rows, :].astype(F32))
    gen = -fock_ref[...] / hess_ref[...]
    square = jnp.sum(jnp.sum(gen * gen, axis=0, keepdims=True), axis=1, keepdims=True)
    rot = gen * jnp.minimum(1.0, math.sqrt(n_occ) / jnp.sqrt(square))
    rot_b = rot.astype(BF16)
    rot_ref[...] = rot_b
    over = matmul(rot_b, rot_b, NT)
    over_b = over.astype(BF16)
    over2 = matmul(over_b, over_b, NN)
    over_rot = matmul(over_b, rot_b, NN)
    eye = jnp.where(
        lax.broadcasted_iota(jnp.int32, (n_occ, n_occ), 0) == lax.broadcasted_iota(jnp.int32, (n_occ, n_occ), 1),
        1.0, 0.0)
    u_oo = (eye - over / 2.0 + over2 / 24.0).astype(BF16)
    u_ref[:, :base] = u_oo[:, :base]
    u_ref[:, base:] = (rot - over_rot / 6.0).astype(BF16)
    u_ref[:, base:n_occ] = u_oo[:, base:]
    l_oo = (over / 6.0 - eye).astype(BF16)
    left_ref[:, :base] = l_oo[:, :base]
    left_ref[:, base:] = (over_rot / 24.0 - rot / 2.0).astype(BF16)
    left_ref[:, base:n_occ] = l_oo[:, base:]
    chosen = matmul(sel_ref[...], u_ref[...], NN)
    chosen_ref[...] = chosen.T[:n_mo].astype(BF16)


def swap_rows(tiles):
    row = lax.broadcasted_iota(jnp.int32, tiles[0].shape, 0)
    for step in (1, 2, 4):
        low = (row // step) % 2 == 0
        after = list(tiles)
        for t in range(8):
            if t & step == 0:
                first, second = tiles[t], tiles[t | step]
                after[t] = jnp.where(low, first, pltpu.roll(second, step, 0))
                after[t | step] = jnp.where(low, pltpu.roll(first, 8 - step, 0), second)
        tiles = after
    return tiles


def half_kernel(n_rows, main, chosen_ref, three_ref, sent_ref, rem_ref, half_ref):
    q_loc, r_loc, n_mo = three_ref.shape
    rem = r_loc - main
    n_dev, dest_rows = sent_ref.shape[:2]
    for q in range(q_loc):
        product = matmul(three_ref[q], chosen_ref[...], NN)
        half_ref[q] = product[:main].T
        rem_ref[q * rem : (q + 1) * rem, :] = product[main:]
    turned = rem_ref[...].T

    def group(at, dest):
        tile, k = divmod(at, n_rows)
        if tile < main // LANES:
            rows = slice(k * n_dev + dest, k * n_dev + dest + 8)
            return swap_rows([half_ref[q, rows, tile * LANES : (tile + 1) * LANES] for q in range(q_loc)])
        zero = jnp.zeros((8, LANES), F32)
        if at > main // LANES * n_rows:
            return [zero] * 8
        rest = [turned[k * n_dev + dest : k * n_dev + dest + 8, :] for k in range(n_rows)]
        return swap_rows(rest + [zero] * (8 - n_rows))

    for dest in range(0, n_dev, 8):
        for at in range(0, dest_rows // 8, 2):
            for d, pair in enumerate(zip(group(at, dest), group(at + 1, dest))):
                sent_ref[dest + d, at * 8 : at * 8 + 16, :] = jnp.concatenate(pair, 0).astype(BF16)


def owner_kernel(n_rows, n_aux, q_loc, r_loc, main, got_ref, left_ref, rot_ref, out_ref):
    n_orb = got_ref.shape[1]
    places = pl.ds(pl.program_id(0) * n_aux, n_aux)
    n_occ, wide = left_ref.shape
    width = rot_ref.shape[1]
    base = wide - width
    n_mo = n_orb * r_loc
    n_vir = n_mo - n_occ
    rem = r_loc - main
    group = n_rows * q_loc
    rows = n_aux * group
    lane_q = lax.broadcasted_iota(jnp.int32, (n_aux, q_loc, LANES), 2) // rem
    own_q = lane_q == lax.broadcasted_iota(jnp.int32, (n_aux, q_loc, LANES), 1)
    e_row = lax.broadcasted_iota(jnp.int32, (LANES, LANES), 0) % rem
    e_col = lax.broadcasted_iota(jnp.int32, (LANES, LANES), 1)

    sources = []
    rest = jnp.zeros((rows, LANES), F32)
    for b in range(n_orb):
        block = got_ref[places, b, :, :].astype(F32)
        pieces = [block[:, c * group : (c + 1) * group, :].reshape(rows, LANES) for c in range(main // LANES)]
        last = main // LANES * group
        spread = [
            jnp.where(own_q, jnp.broadcast_to(block[:, last + k : last + k + 1, :], own_q.shape), 0.0)
            for k in range(n_rows)
        ]
        spread = jnp.concatenate(spread, 1).reshape(rows, LANES).astype(BF16)
        rest = rest + matmul(spread, jnp.where(e_row + b * rem == e_col, 1.0, 0.0).astype(BF16), NN)
        sources.append((lambda tile, pieces=pieces: pieces[tile], 0, b * r_loc, main))
    for b in range(n_orb):
        sources.append((lambda tile: rest, b * rem, b * r_loc + main, rem))
    sources.sort(key=lambda entry: entry[2])
    half = jnp.concatenate(assemble(sources, wide, rows), 1)
    inner = matmul(half.astype(BF16), left_ref[...], NT).astype(BF16)
    total = half[:, base:] + matmul(inner, rot_ref[...], NN)
    total = total.reshape(n_aux, group, width)
    per_row = [total[:, k * q_loc : (k + 1) * q_loc, :].reshape(n_aux * q_loc, width) for k in range(n_rows)]
    sources = [
        (lambda tile, value=value: value[:, tile * LANES : (tile + 1) * LANES], n_occ - base, k * n_vir, n_vir)
        for k, value in enumerate(per_row)
    ]
    length = n_rows * n_vir
    for at, value in enumerate(assemble(sources, length, n_aux * q_loc)):
        stop = min(length, (at + 1) * LANES)
        out_ref[:, at * LANES : stop] = value[:, : stop - at * LANES].astype(BF16)


def on_device(n_aux, n_orb, three_index, density, hess_diag):
    n_dev = n_aux * n_orb
    q_loc, r_loc, n_mo = three_index.shape
    n_occ = density.shape[2]
    n_vir = n_mo - n_occ
    occ_blk = n_occ // n_orb
    pairs = occ_blk * n_vir // n_aux
    base = n_occ // LANES * LANES
    tiles = -(-(n_mo - base) // LANES)
    width = tiles * LANES
    main = r_loc // LANES * LANES
    assert n_dev & (n_dev - 1) == 0 and n_dev >= 8 and tiles % 4 == 0
    tracks = tracks_of(n_dev)
    whole = lambda *shape: pl.BlockSpec(shape, lambda *_: (0,) * len(shape))
    in_vmem = pl.BlockSpec(memory_space=pltpu.VMEM)

    half_shape = (2, tiles * n_occ // 8, LANES)
    in_hbm = pl.BlockSpec(memory_space=pltpu.HBM)
    *parts, three_vmem = pl.pallas_call(
        functools.partial(fock_kernel, n_orb, n_dev, tracks),
        in_specs=[in_hbm, in_vmem],
        out_specs=[in_vmem] * 5,
        out_shape=[
            jax.ShapeDtypeStruct(half_shape, F32),
            jax.ShapeDtypeStruct(half_shape, F32),
            jax.ShapeDtypeStruct(half_shape, BF16),
            jax.ShapeDtypeStruct(half_shape, BF16),
            jax.ShapeDtypeStruct(three_index.shape, BF16),
        ],
        scratch_shapes=[
            pltpu.VMEM((tiles * n_occ, LANES), F32),
            pltpu.SemaphoreType.DMA((q_loc,)),
        ],
        compiler_params=pltpu.CompilerParams(vmem_limit_bytes=38 * MIB),
        cost_estimate=pl.CostEstimate(
            flops=2 * q_loc * r_loc * n_occ * n_mo, bytes_accessed=2 * q_loc * r_loc * n_mo, transcendentals=0),
        name="fock",
    )(three_index, density.transpose(0, 2, 1))
    hess = jnp.pad(
        hess_diag.T, ((0, 0), (n_occ - base, width - (n_mo - base))), constant_values=jnp.inf)

    masks = [[1 | 1 << tracks[half_of(d, n_dev)][k] for d in range(n_dev)] for k in range(len(tracks[0]))]
    held, other = [], []
    for chain in (0, 1):
        part = parts[chain] + swap(parts[2 + chain], [1] * n_dev).astype(F32)
        piece = part[0] + swap(part[1].astype(BF16), masks[0]).astype(F32)
        for mask in masks[1:]:
            piece = piece + swap(piece.astype(BF16), mask).astype(F32)
        piece = piece.astype(BF16)
        held.append(jnp.stack([piece, swap(piece, masks[0])]))
        other.append(swap(held[chain], [1] * n_dev))

    assert q_loc == 8
    first = [p * pairs // n_vir for p in range(n_aux)]
    n_rows = max(-(-(p + 1) * pairs // n_vir) - first[p] for p in range(n_aux))
    sel = np.zeros((n_rows, n_aux, n_orb, n_occ), np.float32)
    for k in range(n_rows):
        for p in range(n_aux):
            for b in range(n_orb):
                sel[k, p, b, b * occ_blk + min(first[p] + k, occ_blk - 1)] = 1.0
    sel = jnp.asarray(sel.reshape(n_rows * n_dev, n_occ), BF16)

    dest_rows = -(-(main // LANES * n_rows * q_loc + n_rows) // 16) * 16
    wide = base + width
    chosen, left, rot = pl.pallas_call(
        functools.partial(rotation_kernel, n_orb, n_dev, tracks),
        in_specs=[in_vmem] * 6,
        out_specs=[in_vmem] * 3,
        out_shape=[
            jax.ShapeDtypeStruct((n_mo, n_rows * n_dev), BF16),
            jax.ShapeDtypeStruct((n_occ, wide), BF16),
            jax.ShapeDtypeStruct((n_occ, width), BF16),
        ],
        scratch_shapes=[pltpu.VMEM((n_occ, width), F32), pltpu.VMEM((n_occ, wide), BF16)],
        compiler_params=pltpu.CompilerParams(vmem_limit_bytes=16 * MIB),
        cost_estimate=pl.CostEstimate(flops=8 * n_occ * n_occ * n_mo, bytes_accessed=4 * MIB, transcendentals=0),
        name="rotation",
    )(*held, *other, hess, sel)
    sent = pl.pallas_call(
        functools.partial(half_kernel, n_rows, main),
        in_specs=[in_vmem] * 2,
        out_specs=in_vmem,
        out_shape=jax.ShapeDtypeStruct((n_dev, dest_rows, LANES), BF16),
        scratch_shapes=[
            pltpu.VMEM((q_loc * (r_loc - main), n_rows * n_dev), F32),
            pltpu.VMEM((q_loc, n_rows * n_dev, main), F32),
        ],
        compiler_params=pltpu.CompilerParams(vmem_limit_bytes=40 * MIB),
        cost_estimate=pl.CostEstimate(
            flops=2 * q_loc * r_loc * n_rows * n_dev * n_mo, bytes_accessed=2 * q_loc * r_loc * n_mo, transcendentals=0),
        name="half_rotation",
    )(chosen, three_vmem)

    got = lax.all_to_all(sent, BOTH, 0, 0, tiled=True).reshape(n_aux, n_orb, dest_rows, LANES)
    aux_step = min(n_aux, 8)
    out = pl.pallas_call(
        functools.partial(owner_kernel, n_rows, aux_step, q_loc, r_loc, main),
        grid=(n_aux // aux_step,),
        in_specs=[in_vmem] * 3,
        out_specs=pl.BlockSpec((aux_step * q_loc, n_rows * n_vir), lambda g: (g, 0)),
        out_shape=jax.ShapeDtypeStruct((n_aux * q_loc, n_rows * n_vir), BF16),
        compiler_params=pltpu.CompilerParams(vmem_limit_bytes=40 * MIB),
        cost_estimate=pl.CostEstimate(
            flops=4 * n_aux * q_loc * n_rows * n_occ * n_mo, bytes_accessed=8 * MIB, transcendentals=0),
        name="owner_rows",
    )(got, left, rot)
    if n_rows * n_vir != pairs:
        start = (lax.axis_index("aux") * pairs) % n_vir
        out = lax.dynamic_slice_in_dim(out, start, pairs, 1)
    return out[None]


def solution(mesh):
    def body(*args):
        return on_device(mesh.shape["aux"], mesh.shape["orb"], *args)

    return jax.shard_map(
        body,
        mesh=mesh,
        in_specs=(P("aux", "orb", None), P("aux", "orb", None), P()),
        out_specs=P("orb", None, "aux"),
        check_vma=False,
    )
```

```python
import functools
import math

import jax
import jax.numpy as jnp
import numpy as np
from jax import lax
from jax.experimental import pallas as pl
from jax.experimental.pallas import tpu as pltpu
from jax.sharding import PartitionSpec as P

BOTH = ("aux", "orb")
F32 = jnp.float32
BF16 = jnp.bfloat16
LANES = 128
MIB = 1 << 20


def matmul(a, b, dims):
    return lax.dot_general(a, b, (dims, ((), ())), preferred_element_type=F32)


NN = ((1,), (0,))
NT = ((1,), (1,))
TN = ((0,), (0,))


def my_index(n_orb):
    return lax.axis_index("aux") * n_orb + lax.axis_index("orb")


def swap(x, masks):
    return lax.ppermute(x, BOTH, [(d, d ^ mask) for d, mask in enumerate(masks)])


def tracks_of(n_dev):
    bits = n_dev.bit_length() - 1
    return [1, 2, *range(3, bits)], [2, 1, *range(bits - 1, 2, -1)]


def bit(index, which):
    return (index // (1 << which)) % 2


def half_of(index, n_dev):
    return sum(bit(index, k) for k in range(n_dev.bit_length() - 1)) % 2


def assemble(sources, width, rows):
    lane = lax.broadcasted_iota(jnp.int32, (rows, LANES), 1)
    rolled = {}

    def source_tile(which, tile, turn):
        key = (which, tile, turn)
        if key not in rolled:
            value = sources[which][0](tile)
            rolled[key] = pltpu.roll(value, turn, 1) if turn else value
        return rolled[key]

    tiles = []
    for start in range(0, width, LANES):
        result, end_done = None, 0
        for which, (_, src, dst, count) in enumerate(sources):
            low, high = max(dst, start), min(dst + count, start + LANES)
            turn = (dst - src) % LANES
            at = low
            while at < high:
                from_lane = at - dst + src
                tile = from_lane // LANES
                stop = min(high, at + LANES - from_lane % LANES)
                value = source_tile(which, tile, turn)
                if result is None:
                    result = value
                    if at > start:
                        result = jnp.where(lane >= at - start, value, 0.0)
                else:
                    result = jnp.where(lane >= at - start, value, result)
                end_done = stop - start
                at = stop
        if end_done < LANES:
            result = jnp.where(lane < end_done, result, 0.0)
        tiles.append(result)
    return tiles


def load_kernel(three_hbm, three_ref, sems):
    copies = [
        pltpu.make_async_copy(three_hbm.at[q], three_ref.at[q], sems.at[q]) for q in range(three_ref.shape[0])
    ]
    for copy in copies:
        copy.start()
    for copy in copies:
        copy.wait()


def fock_half(side, lead, n_rows, base, slices, ready, dens_ref, part_refs, acc_ref):
    n_occ = dens_ref.shape[1]
    n_tiles = acc_ref.shape[0] // n_occ
    for static in (0, 1):

        @pl.when(side == static)
        def _(static=static):
            low = base + static * n_tiles * LANES
            for q, three in enumerate(slices):
                ready(q)
                high = min(three.shape[1], low + n_tiles * LANES)
                part = matmul(dens_ref[q], three[:, low:high], NN)
                for t in range(n_tiles):
                    stop = min(LANES, high - low - t * LANES)
                    rows = slice(t * n_occ, (t + 1) * n_occ)
                    piece = part[:, t * LANES : t * LANES + stop]
                    if q:
                        acc_ref[rows, :stop] += piece
                    else:
                        if stop < LANES:
                            acc_ref[rows, :] = jnp.zeros((n_occ, LANES), F32)
                        acc_ref[rows, :stop] = piece

    for chain, ref in enumerate(part_refs):
        for j in (0, 1):
            start = pl.multiple_of((chain * 2 + (lead + j) % 2) * n_rows, n_rows)
            ref[j] = acc_ref[pl.ds(start, n_rows), :].astype(ref.dtype)


def side_and_lead(own, n_orb, n_dev, tracks):
    me = my_index(n_orb)
    side = half_of(me, n_dev) if own else 1 - half_of(me, n_dev)
    return side, jnp.where(side == 0, bit(me, tracks[0][0]), bit(me, tracks[1][0]))


def send_kernel(n_orb, n_dev, tracks, n_rows, base, three_hbm, first_ref, dens_ref,
                part_0, part_1, last_ref, acc_ref, sems):
    n_first, n_last = first_ref.shape[0], last_ref.shape[0]
    copies = [
        pltpu.make_async_copy(three_hbm.at[n_first + q], last_ref.at[q], sems.at[q]) for q in range(n_last)
    ]
    for copy in copies:
        copy.start()
    slices = [first_ref.at[q] for q in range(n_first)] + [last_ref.at[q] for q in range(n_last)]

    def ready(q):
        if q >= n_first:
            copies[q - n_first].wait()

    side, lead = side_and_lead(False, n_orb, n_dev, tracks)
    fock_half(side, lead, n_rows, base, slices, ready, dens_ref, (part_0, part_1), acc_ref)


def keep_kernel(n_orb, n_dev, tracks, n_rows, base, first_ref, last_ref, dens_ref, part_0, part_1, acc_ref):
    slices = [ref.at[q] for ref in (first_ref, last_ref) for q in range(ref.shape[0])]
    side, lead = side_and_lead(True, n_orb, n_dev, tracks)
    fock_half(side, lead, n_rows, base, slices, lambda q: None, dens_ref, (part_0, part_1), acc_ref)


def rotation_kernel(n_orb, n_dev, tracks, mine_0, mine_1, other_0, other_1, hess_ref, sel_ref, chosen_ref, left_ref, rot_ref, fock_ref, u_ref):
    n_occ, width = fock_ref.shape
    base = n_occ // LANES * LANES
    n_mo = chosen_ref.shape[0]
    mine_refs, other_refs = (mine_0, mine_1), (other_0, other_1)
    n_rows = mine_0.shape[1]
    step = math.gcd(n_rows, n_occ)
    me = my_index(n_orb)
    mine = half_of(me, n_dev)
    for start in range(0, 8 * n_rows, step):
        tile, row = divmod(start, n_occ)
        piece, at = divmod(start, n_rows)
        side, chain, j = piece // 4, piece // 2 % 2, piece % 2
        place = (j + bit(me, tracks[side][0])) % 2
        rows = slice(at, at + step)
        fock_ref[row : row + step, tile * LANES : (tile + 1) * LANES] = jnp.where(
            mine == side, mine_refs[chain][place, rows, :].astype(F32), other_refs[chain][place, rows, :].astype(F32))
    gen = -fock_ref[...] / hess_ref[...]
    square = jnp.sum(jnp.sum(gen * gen, axis=0, keepdims=True), axis=1, keepdims=True)
    rot = gen * jnp.minimum(1.0, math.sqrt(n_occ) / jnp.sqrt(square))
    rot_b = rot.astype(BF16)
    rot_ref[...] = rot_b
    over = matmul(rot_b, rot_b, NT)
    over_b = over.astype(BF16)
    over2 = matmul(over_b, over_b, NN)
    over_rot = matmul(over_b, rot_b, NN)
    eye = jnp.where(
        lax.broadcasted_iota(jnp.int32, (n_occ, n_occ), 0) == lax.broadcasted_iota(jnp.int32, (n_occ, n_occ), 1),
        1.0, 0.0)
    u_oo = (eye - over / 2.0 + over2 / 24.0).astype(BF16)
    u_ref[:, :base] = u_oo[:, :base]
    u_ref[:, base:] = (rot - over_rot / 6.0).astype(BF16)
    u_ref[:, base:n_occ] = u_oo[:, base:]
    l_oo = (over / 6.0 - eye).astype(BF16)
    left_ref[:, :base] = l_oo[:, :base]
    left_ref[:, base:] = (over_rot / 24.0 - rot / 2.0).astype(BF16)
    left_ref[:, base:n_occ] = l_oo[:, base:]
    chosen = matmul(sel_ref[...], u_ref[...], NN)
    chosen_ref[...] = chosen.T[:n_mo].astype(BF16)


def swap_rows(tiles):
    row = lax.broadcasted_iota(jnp.int32, tiles[0].shape, 0)
    for step in (1, 2, 4):
        low = (row // step) % 2 == 0
        after = list(tiles)
        for t in range(8):
            if t & step == 0:
                first, second = tiles[t], tiles[t | step]
                after[t] = jnp.where(low, first, pltpu.roll(second, step, 0))
                after[t | step] = jnp.where(low, pltpu.roll(first, 8 - step, 0), second)
        tiles = after
    return tiles


def half_kernel(n_rows, main, chosen_ref, first_ref, last_ref, sent_ref, rem_ref, half_ref):
    slices = [ref.at[q] for ref in (first_ref, last_ref) for q in range(ref.shape[0])]
    q_loc, r_loc = len(slices), first_ref.shape[1]
    rem = r_loc - main
    n_dev, dest_rows = sent_ref.shape[:2]
    for q in range(q_loc):
        product = matmul(slices[q][...], chosen_ref[...], NN)
        half_ref[q] = product[:main].T
        rem_ref[q * rem : (q + 1) * rem, :] = product[main:]
    turned = rem_ref[...].T

    def group(at, dest):
        tile, k = divmod(at, n_rows)
        if tile < main // LANES:
            rows = slice(k * n_dev + dest, k * n_dev + dest + 8)
            return swap_rows([half_ref[q, rows, tile * LANES : (tile + 1) * LANES] for q in range(q_loc)])
        zero = jnp.zeros((8, LANES), F32)
        if at > main // LANES * n_rows:
            return [zero] * 8
        rest = [turned[k * n_dev + dest : k * n_dev + dest + 8, :] for k in range(n_rows)]
        return swap_rows(rest + [zero] * (8 - n_rows))

    for dest in range(0, n_dev, 8):
        for at in range(0, dest_rows // 8, 2):
            for d, pair in enumerate(zip(group(at, dest), group(at + 1, dest))):
                sent_ref[dest + d, at * 8 : at * 8 + 16, :] = jnp.concatenate(pair, 0).astype(BF16)


def owner_kernel(n_rows, n_aux, q_loc, r_loc, main, got_ref, left_ref, rot_ref, out_ref):
    n_orb = got_ref.shape[1]
    places = pl.ds(pl.program_id(0) * n_aux, n_aux)
    n_occ, wide = left_ref.shape
    width = rot_ref.shape[1]
    base = wide - width
    n_mo = n_orb * r_loc
    n_vir = n_mo - n_occ
    rem = r_loc - main
    group = n_rows * q_loc
    rows = n_aux * group
    lane_q = lax.broadcasted_iota(jnp.int32, (n_aux, q_loc, LANES), 2) // rem
    own_q = lane_q == lax.broadcasted_iota(jnp.int32, (n_aux, q_loc, LANES), 1)
    e_row = lax.broadcasted_iota(jnp.int32, (LANES, LANES), 0) % rem
    e_col = lax.broadcasted_iota(jnp.int32, (LANES, LANES), 1)

    sources = []
    rest = jnp.zeros((rows, LANES), F32)
    for b in range(n_orb):
        block = got_ref[places, b, :, :].astype(F32)
        pieces = [block[:, c * group : (c + 1) * group, :].reshape(rows, LANES) for c in range(main // LANES)]
        last = main // LANES * group
        spread = [
            jnp.where(own_q, jnp.broadcast_to(block[:, last + k : last + k + 1, :], own_q.shape), 0.0)
            for k in range(n_rows)
        ]
        spread = jnp.concatenate(spread, 1).reshape(rows, LANES).astype(BF16)
        rest = rest + matmul(spread, jnp.where(e_row + b * rem == e_col, 1.0, 0.0).astype(BF16), NN)
        sources.append((lambda tile, pieces=pieces: pieces[tile], 0, b * r_loc, main))
    for b in range(n_orb):
        sources.append((lambda tile: rest, b * rem, b * r_loc + main, rem))
    sources.sort(key=lambda entry: entry[2])
    half = jnp.concatenate(assemble(sources, wide, rows), 1)
    inner = matmul(half.astype(BF16), left_ref[...], NT).astype(BF16)
    total = half[:, base:] + matmul(inner, rot_ref[...], NN)
    total = total.reshape(n_aux, group, width)
    per_row = [total[:, k * q_loc : (k + 1) * q_loc, :].reshape(n_aux * q_loc, width) for k in range(n_rows)]
    sources = [
        (lambda tile, value=value: value[:, tile * LANES : (tile + 1) * LANES], n_occ - base, k * n_vir, n_vir)
        for k, value in enumerate(per_row)
    ]
    length = n_rows * n_vir
    for at, value in enumerate(assemble(sources, length, n_aux * q_loc)):
        stop = min(length, (at + 1) * LANES)
        out_ref[:, at * LANES : stop] = value[:, : stop - at * LANES].astype(BF16)


def on_device(n_aux, n_orb, three_index, density, hess_diag):
    n_dev = n_aux * n_orb
    q_loc, r_loc, n_mo = three_index.shape
    n_occ = density.shape[2]
    n_vir = n_mo - n_occ
    occ_blk = n_occ // n_orb
    pairs = occ_blk * n_vir // n_aux
    base = n_occ // LANES * LANES
    tiles = -(-(n_mo - base) // LANES)
    width = tiles * LANES
    main = r_loc // LANES * LANES
    assert n_dev & (n_dev - 1) == 0 and n_dev >= 8 and tiles % 4 == 0
    tracks = tracks_of(n_dev)
    whole = lambda *shape: pl.BlockSpec(shape, lambda *_: (0,) * len(shape))
    in_vmem = pl.BlockSpec(memory_space=pltpu.VMEM)

    half_shape = (2, tiles * n_occ // 8, LANES)
    in_hbm = pl.BlockSpec(memory_space=pltpu.HBM)
    n_first = q_loc // 2
    n_last = q_loc - n_first
    piece_rows = tiles * n_occ // 8
    acc = pltpu.VMEM((tiles // 2 * n_occ, LANES), F32)
    cost = lambda flops, moved: pl.CostEstimate(flops=flops, bytes_accessed=moved, transcendentals=0)
    three_a = pl.pallas_call(
        load_kernel,
        in_specs=[in_hbm],
        out_specs=in_vmem,
        out_shape=jax.ShapeDtypeStruct((n_first, r_loc, n_mo), BF16),
        scratch_shapes=[pltpu.SemaphoreType.DMA((n_first,))],
        compiler_params=pltpu.CompilerParams(vmem_limit_bytes=43 * MIB),
        cost_estimate=cost(0, 4 * n_first * r_loc * n_mo),
        name="load",
    )(three_index)
    dens = density.transpose(0, 2, 1)
    *send, three_b = pl.pallas_call(
        functools.partial(send_kernel, n_orb, n_dev, tracks, piece_rows, base),
        in_specs=[in_hbm, in_vmem, in_vmem],
        out_specs=[in_vmem] * 3,
        out_shape=[
            jax.ShapeDtypeStruct(half_shape, BF16),
            jax.ShapeDtypeStruct(half_shape, BF16),
            jax.ShapeDtypeStruct((n_last, r_loc, n_mo), BF16),
        ],
        scratch_shapes=[acc, pltpu.SemaphoreType.DMA((n_last,))],
        compiler_params=pltpu.CompilerParams(vmem_limit_bytes=39 * MIB),
        cost_estimate=cost(q_loc * r_loc * n_occ * n_mo, 4 * n_last * r_loc * n_mo),
        name="fock_sent",
    )(three_index, three_a, dens)
    keep = pl.pallas_call(
        functools.partial(keep_kernel, n_orb, n_dev, tracks, piece_rows, base),
        in_specs=[in_vmem] * 3,
        out_specs=[in_vmem] * 2,
        out_shape=[jax.ShapeDtypeStruct(half_shape, F32)] * 2,
        scratch_shapes=[acc],
        compiler_params=pltpu.CompilerParams(vmem_limit_bytes=16 * MIB),
        cost_estimate=cost(q_loc * r_loc * n_occ * n_mo, MIB),
        name="fock_kept",
    )(three_a, three_b, dens)
    hess = jnp.pad(
        hess_diag.T, ((0, 0), (n_occ - base, width - (n_mo - base))), constant_values=jnp.inf)

    masks = [[1 | 1 << tracks[half_of(d, n_dev)][k] for d in range(n_dev)] for k in range(len(tracks[0]))]
    held, other = [], []
    for chain in (0, 1):
        part = keep[chain] + swap(send[chain], [1] * n_dev).astype(F32)
        piece = part[0] + swap(part[1].astype(BF16), masks[0]).astype(F32)
        for mask in masks[1:]:
            piece = piece + swap(piece.astype(BF16), mask).astype(F32)
        piece = piece.astype(BF16)
        held.append(jnp.stack([piece, swap(piece, masks[0])]))
        other.append(swap(held[chain], [1] * n_dev))

    assert q_loc == 8
    first = [p * pairs // n_vir for p in range(n_aux)]
    n_rows = max(-(-(p + 1) * pairs // n_vir) - first[p] for p in range(n_aux))
    sel = np.zeros((n_rows, n_aux, n_orb, n_occ), np.float32)
    for k in range(n_rows):
        for p in range(n_aux):
            for b in range(n_orb):
                sel[k, p, b, b * occ_blk + min(first[p] + k, occ_blk - 1)] = 1.0
    sel = jnp.asarray(sel.reshape(n_rows * n_dev, n_occ), BF16)

    dest_rows = -(-(main // LANES * n_rows * q_loc + n_rows) // 16) * 16
    wide = base + width
    chosen, left, rot = pl.pallas_call(
        functools.partial(rotation_kernel, n_orb, n_dev, tracks),
        in_specs=[in_vmem] * 6,
        out_specs=[in_vmem] * 3,
        out_shape=[
            jax.ShapeDtypeStruct((n_mo, n_rows * n_dev), BF16),
            jax.ShapeDtypeStruct((n_occ, wide), BF16),
            jax.ShapeDtypeStruct((n_occ, width), BF16),
        ],
        scratch_shapes=[pltpu.VMEM((n_occ, width), F32), pltpu.VMEM((n_occ, wide), BF16)],
        compiler_params=pltpu.CompilerParams(vmem_limit_bytes=16 * MIB),
        cost_estimate=pl.CostEstimate(flops=8 * n_occ * n_occ * n_mo, bytes_accessed=4 * MIB, transcendentals=0),
        name="rotation",
    )(*held, *other, hess, sel)
    sent = pl.pallas_call(
        functools.partial(half_kernel, n_rows, main),
        in_specs=[in_vmem] * 3,
        out_specs=in_vmem,
        out_shape=jax.ShapeDtypeStruct((n_dev, dest_rows, LANES), BF16),
        scratch_shapes=[
            pltpu.VMEM((q_loc * (r_loc - main), n_rows * n_dev), F32),
            pltpu.VMEM((q_loc, n_rows * n_dev, main), F32),
        ],
        compiler_params=pltpu.CompilerParams(vmem_limit_bytes=40 * MIB),
        cost_estimate=pl.CostEstimate(
            flops=2 * q_loc * r_loc * n_rows * n_dev * n_mo, bytes_accessed=2 * q_loc * r_loc * n_mo, transcendentals=0),
        name="half_rotation",
    )(chosen, three_a, three_b)

    got = lax.all_to_all(sent, BOTH, 0, 0, tiled=True).reshape(n_aux, n_orb, dest_rows, LANES)
    aux_step = min(n_aux, 8)
    out = pl.pallas_call(
        functools.partial(owner_kernel, n_rows, aux_step, q_loc, r_loc, main),
        grid=(n_aux // aux_step,),
        in_specs=[in_vmem] * 3,
        out_specs=pl.BlockSpec((aux_step * q_loc, n_rows * n_vir), lambda g: (g, 0)),
        out_shape=jax.ShapeDtypeStruct((n_aux * q_loc, n_rows * n_vir), BF16),
        compiler_params=pltpu.CompilerParams(vmem_limit_bytes=40 * MIB),
        cost_estimate=pl.CostEstimate(
            flops=4 * n_aux * q_loc * n_rows * n_occ * n_mo, bytes_accessed=8 * MIB, transcendentals=0),
        name="owner_rows",
    )(got, left, rot)
    if n_rows * n_vir != pairs:
        start = (lax.axis_index("aux") * pairs) % n_vir
        out = lax.dynamic_slice_in_dim(out, start, pairs, 1)
    return out[None]


def solution(mesh):
    def body(*args):
        return on_device(mesh.shape["aux"], mesh.shape["orb"], *args)

    return jax.shard_map(
        body,
        mesh=mesh,
        in_specs=(P("aux", "orb", None), P("aux", "orb", None), P()),
        out_specs=P("orb", None, "aux"),
        check_vma=False,
    )
```

```python
import functools
import math

import jax
import jax.numpy as jnp
import numpy as np
from jax import lax
from jax.experimental import pallas as pl
from jax.experimental.pallas import tpu as pltpu
from jax.sharding import PartitionSpec as P

BOTH = ("aux", "orb")
F32 = jnp.float32
BF16 = jnp.bfloat16
LANES = 128
MIB = 1 << 20


def matmul(a, b, dims):
    return lax.dot_general(a, b, (dims, ((), ())), preferred_element_type=F32)


NN = ((1,), (0,))
NT = ((1,), (1,))
TN = ((0,), (0,))


def to_hbm(x):
    return pltpu.with_memory_space_constraint(x, pltpu.HBM)


def my_index(n_orb):
    return lax.axis_index("aux") * n_orb + lax.axis_index("orb")


def swap(x, masks):
    return lax.ppermute(x, BOTH, [(d, d ^ mask) for d, mask in enumerate(masks)])


def tracks_of(n_dev):
    bits = n_dev.bit_length() - 1
    return [1, 2, *range(3, bits)], [2, 1, *range(bits - 1, 2, -1)]


def bit(index, which):
    return (index // (1 << which)) % 2


def half_of(index, n_dev):
    return sum(bit(index, k) for k in range(n_dev.bit_length() - 1)) % 2


def assemble(sources, width, rows):
    lane = lax.broadcasted_iota(jnp.int32, (rows, LANES), 1)
    rolled = {}

    def source_tile(which, tile, turn):
        key = (which, tile, turn)
        if key not in rolled:
            value = sources[which][0](tile)
            rolled[key] = pltpu.roll(value, turn, 1) if turn else value
        return rolled[key]

    tiles = []
    for start in range(0, width, LANES):
        result, end_done = None, 0
        for which, (_, src, dst, count) in enumerate(sources):
            low, high = max(dst, start), min(dst + count, start + LANES)
            turn = (dst - src) % LANES
            at = low
            while at < high:
                from_lane = at - dst + src
                tile = from_lane // LANES
                stop = min(high, at + LANES - from_lane % LANES)
                value = source_tile(which, tile, turn)
                if result is None:
                    result = value
                    if at > start:
                        result = jnp.where(lane >= at - start, value, 0.0)
                else:
                    result = jnp.where(lane >= at - start, value, result)
                end_done = stop - start
                at = stop
        if end_done < LANES:
            result = jnp.where(lane < end_done, result, 0.0)
        tiles.append(result)
    return tiles


def fock_kernel(n_orb, n_dev, tracks, three_hbm, dens_hbm, *refs):
    *part_refs, three_ref, acc_ref, dens_ref, sems, dens_sems = refs
    q_loc, _, n_mo = three_ref.shape
    n_occ = dens_ref.shape[1]
    n_tiles = acc_ref.shape[0] // n_occ
    base = n_occ // LANES * LANES
    copies = []
    for q in range(q_loc):
        copies.append((
            pltpu.make_async_copy(dens_hbm.at[q], dens_ref.at[q], dens_sems.at[q]),
            pltpu.make_async_copy(three_hbm.at[q], three_ref.at[q], sems.at[q]),
        ))
        for copy in copies[q]:
            copy.start()
    for q in range(q_loc):
        for copy in copies[q]:
            copy.wait()
        part = matmul(dens_ref[q], three_ref[q, :, base:], NN)
        for t in range(n_tiles):
            stop = min(LANES, n_mo - base - t * LANES)
            rows = slice(t * n_occ, (t + 1) * n_occ)
            piece = part[:, t * LANES : t * LANES + stop]
            if q:
                acc_ref[rows, :stop] += piece
            else:
                if stop < LANES:
                    acc_ref[rows, :] = jnp.zeros((n_occ, LANES), F32)
                acc_ref[rows, :stop] = piece
    me = my_index(n_orb)
    mine = half_of(me, n_dev)
    n_rows = n_tiles * n_occ // 8
    for chain in (0, 1):
        for ref, side in zip(part_refs[chain::2], (mine, 1 - mine)):
            lead = jnp.where(side == 0, bit(me, tracks[0][0]), bit(me, tracks[1][0]))
            for j in (0, 1):
                start = pl.multiple_of((side * 4 + chain * 2 + (lead + j) % 2) * n_rows, n_rows)
                ref[j] = acc_ref[pl.ds(start, n_rows), :].astype(ref.dtype)


def rotation_kernel(n_orb, n_dev, tracks, mine_0, mine_1, other_0, other_1, hess_ref, sel_ref, chosen_ref, left_ref, rot_ref, fock_ref, u_ref):
    n_occ, width = fock_ref.shape
    base = n_occ // LANES * LANES
    n_mo = chosen_ref.shape[0]
    mine_refs, other_refs = (mine_0, mine_1), (other_0, other_1)
    n_rows = mine_0.shape[1]
    step = math.gcd(n_rows, n_occ)
    me = my_index(n_orb)
    mine = half_of(me, n_dev)
    for start in range(0, 8 * n_rows, step):
        tile, row = divmod(start, n_occ)
        piece, at = divmod(start, n_rows)
        side, chain, j = piece // 4, piece // 2 % 2, piece % 2
        place = (j + bit(me, tracks[side][0])) % 2
        rows = slice(at, at + step)
        fock_ref[row : row + step, tile * LANES : (tile + 1) * LANES] = jnp.where(
            mine == side, mine_refs[chain][place, rows, :].astype(F32), other_refs[chain][place, rows, :].astype(F32))
    gen = -fock_ref[...] / hess_ref[...]
    square = jnp.sum(jnp.sum(gen * gen, axis=0, keepdims=True), axis=1, keepdims=True)
    rot = gen * jnp.minimum(1.0, math.sqrt(n_occ) / jnp.sqrt(square))
    rot_b = rot.astype(BF16)
    rot_ref[...] = rot_b
    over = matmul(rot_b, rot_b, NT)
    over_b = over.astype(BF16)
    over2 = matmul(over_b, over_b, NN)
    over_rot = matmul(over_b, rot_b, NN)
    eye = jnp.where(
        lax.broadcasted_iota(jnp.int32, (n_occ, n_occ), 0) == lax.broadcasted_iota(jnp.int32, (n_occ, n_occ), 1),
        1.0, 0.0)
    u_oo = (eye - over / 2.0 + over2 / 24.0).astype(BF16)
    u_ref[:, :base] = u_oo[:, :base]
    u_ref[:, base:] = (rot - over_rot / 6.0).astype(BF16)
    u_ref[:, base:n_occ] = u_oo[:, base:]
    l_oo = (over / 6.0 - eye).astype(BF16)
    left_ref[:, :base] = l_oo[:, :base]
    left_ref[:, base:] = (over_rot / 24.0 - rot / 2.0).astype(BF16)
    left_ref[:, base:n_occ] = l_oo[:, base:]
    chosen = matmul(sel_ref[...], u_ref[...], NN)
    chosen_ref[...] = chosen.T[:n_mo].astype(BF16)


def swap_rows(tiles):
    row = lax.broadcasted_iota(jnp.int32, tiles[0].shape, 0)
    for step in (1, 2, 4):
        low = (row // step) % 2 == 0
        after = list(tiles)
        for t in range(8):
            if t & step == 0:
                first, second = tiles[t], tiles[t | step]
                after[t] = jnp.where(low, first, pltpu.roll(second, step, 0))
                after[t | step] = jnp.where(low, pltpu.roll(first, 8 - step, 0), second)
        tiles = after
    return tiles


def half_kernel(n_rows, main, chosen_ref, three_ref, sent_ref, rem_ref, half_ref):
    q_loc, r_loc, n_mo = three_ref.shape
    rem = r_loc - main
    n_dev, dest_rows = sent_ref.shape[:2]
    for q in range(q_loc):
        product = matmul(three_ref[q], chosen_ref[...], NN)
        half_ref[q] = product[:main].T
        rem_ref[q * rem : (q + 1) * rem, :] = product[main:]
    turned = rem_ref[...].T

    def group(at, dest):
        tile, k = divmod(at, n_rows)
        if tile < main // LANES:
            rows = slice(k * n_dev + dest, k * n_dev + dest + 8)
            return swap_rows([half_ref[q, rows, tile * LANES : (tile + 1) * LANES] for q in range(q_loc)])
        zero = jnp.zeros((8, LANES), F32)
        if at > main // LANES * n_rows:
            return [zero] * 8
        rest = [turned[k * n_dev + dest : k * n_dev + dest + 8, :] for k in range(n_rows)]
        return swap_rows(rest + [zero] * (8 - n_rows))

    for dest in range(0, n_dev, 8):
        for at in range(0, dest_rows // 8, 2):
            for d, pair in enumerate(zip(group(at, dest), group(at + 1, dest))):
                sent_ref[dest + d, at * 8 : at * 8 + 16, :] = jnp.concatenate(pair, 0).astype(BF16)


def owner_kernel(n_rows, n_aux, q_loc, r_loc, main, got_ref, left_ref, rot_ref, out_ref):
    n_orb = got_ref.shape[1]
    places = pl.ds(pl.program_id(0) * n_aux, n_aux)
    n_occ, wide = left_ref.shape
    width = rot_ref.shape[1]
    base = wide - width
    n_mo = n_orb * r_loc
    n_vir = n_mo - n_occ
    rem = r_loc - main
    group = n_rows * q_loc
    rows = n_aux * group
    lane_q = lax.broadcasted_iota(jnp.int32, (n_aux, q_loc, LANES), 2) // rem
    own_q = lane_q == lax.broadcasted_iota(jnp.int32, (n_aux, q_loc, LANES), 1)
    e_row = lax.broadcasted_iota(jnp.int32, (LANES, LANES), 0) % rem
    e_col = lax.broadcasted_iota(jnp.int32, (LANES, LANES), 1)

    sources = []
    rest = jnp.zeros((rows, LANES), F32)
    for b in range(n_orb):
        block = got_ref[places, b, :, :].astype(F32)
        pieces = [block[:, c * group : (c + 1) * group, :].reshape(rows, LANES) for c in range(main // LANES)]
        last = main // LANES * group
        spread = [
            jnp.where(own_q, jnp.broadcast_to(block[:, last + k : last + k + 1, :], own_q.shape), 0.0)
            for k in range(n_rows)
        ]
        spread = jnp.concatenate(spread, 1).reshape(rows, LANES).astype(BF16)
        rest = rest + matmul(spread, jnp.where(e_row + b * rem == e_col, 1.0, 0.0).astype(BF16), NN)
        sources.append((lambda tile, pieces=pieces: pieces[tile], 0, b * r_loc, main))
    for b in range(n_orb):
        sources.append((lambda tile: rest, b * rem, b * r_loc + main, rem))
    sources.sort(key=lambda entry: entry[2])
    half = jnp.concatenate(assemble(sources, wide, rows), 1)
    inner = matmul(half.astype(BF16), left_ref[...], NT).astype(BF16)
    total = half[:, base:] + matmul(inner, rot_ref[...], NN)
    total = total.reshape(n_aux, group, width)
    per_row = [total[:, k * q_loc : (k + 1) * q_loc, :].reshape(n_aux * q_loc, width) for k in range(n_rows)]
    sources = [
        (lambda tile, value=value: value[:, tile * LANES : (tile + 1) * LANES], n_occ - base, k * n_vir, n_vir)
        for k, value in enumerate(per_row)
    ]
    length = n_rows * n_vir
    for at, value in enumerate(assemble(sources, length, n_aux * q_loc)):
        stop = min(length, (at + 1) * LANES)
        out_ref[:, at * LANES : stop] = value[:, : stop - at * LANES].astype(BF16)


def on_device(n_aux, n_orb, three_index, density, hess_diag):
    n_dev = n_aux * n_orb
    q_loc, r_loc, n_mo = three_index.shape
    n_occ = density.shape[2]
    n_vir = n_mo - n_occ
    occ_blk = n_occ // n_orb
    pairs = occ_blk * n_vir // n_aux
    base = n_occ // LANES * LANES
    tiles = -(-(n_mo - base) // LANES)
    width = tiles * LANES
    main = r_loc // LANES * LANES
    assert n_dev & (n_dev - 1) == 0 and n_dev >= 8 and tiles % 4 == 0
    tracks = tracks_of(n_dev)
    whole = lambda *shape: pl.BlockSpec(shape, lambda *_: (0,) * len(shape))
    in_vmem = pl.BlockSpec(memory_space=pltpu.VMEM)

    half_shape = (2, tiles * n_occ // 8, LANES)
    in_hbm = pl.BlockSpec(memory_space=pltpu.HBM)
    *parts, three_vmem = pl.pallas_call(
        functools.partial(fock_kernel, n_orb, n_dev, tracks),
        in_specs=[in_hbm, in_hbm],
        out_specs=[in_vmem] * 5,
        out_shape=[
            jax.ShapeDtypeStruct(half_shape, F32),
            jax.ShapeDtypeStruct(half_shape, F32),
            jax.ShapeDtypeStruct(half_shape, BF16),
            jax.ShapeDtypeStruct(half_shape, BF16),
            jax.ShapeDtypeStruct(three_index.shape, BF16),
        ],
        scratch_shapes=[
            pltpu.VMEM((tiles * n_occ, LANES), F32),
            pltpu.VMEM((q_loc, n_occ, r_loc), BF16),
            pltpu.SemaphoreType.DMA((q_loc,)),
            pltpu.SemaphoreType.DMA((q_loc,)),
        ],
        compiler_params=pltpu.CompilerParams(vmem_limit_bytes=38 * MIB),
        cost_estimate=pl.CostEstimate(
            flops=2 * q_loc * r_loc * n_occ * n_mo, bytes_accessed=2 * q_loc * r_loc * n_mo, transcendentals=0),
        name="fock",
    )(to_hbm(three_index), to_hbm(density.transpose(0, 2, 1)))
    hess = jnp.pad(
        hess_diag.T, ((0, 0), (n_occ - base, width - (n_mo - base))), constant_values=jnp.inf)

    masks = [[1 | 1 << tracks[half_of(d, n_dev)][k] for d in range(n_dev)] for k in range(len(tracks[0]))]
    held, other = [], []
    for chain in (0, 1):
        part = parts[chain] + swap(parts[2 + chain], [1] * n_dev).astype(F32)
        piece = part[0] + swap(part[1].astype(BF16), masks[0]).astype(F32)
        for mask in masks[1:]:
            piece = piece + swap(piece.astype(BF16), mask).astype(F32)
        piece = piece.astype(BF16)
        held.append(jnp.stack([piece, swap(piece, masks[0])]))
        other.append(swap(held[chain], [1] * n_dev))

    assert q_loc == 8
    first = [p * pairs // n_vir for p in range(n_aux)]
    n_rows = max(-(-(p + 1) * pairs // n_vir) - first[p] for p in range(n_aux))
    sel = np.zeros((n_rows, n_aux, n_orb, n_occ), np.float32)
    for k in range(n_rows):
        for p in range(n_aux):
            for b in range(n_orb):
                sel[k, p, b, b * occ_blk + min(first[p] + k, occ_blk - 1)] = 1.0
    sel = jnp.asarray(sel.reshape(n_rows * n_dev, n_occ), BF16)

    dest_rows = -(-(main // LANES * n_rows * q_loc + n_rows) // 16) * 16
    wide = base + width
    chosen, left, rot = pl.pallas_call(
        functools.partial(rotation_kernel, n_orb, n_dev, tracks),
        in_specs=[in_vmem] * 6,
        out_specs=[in_vmem] * 3,
        out_shape=[
            jax.ShapeDtypeStruct((n_mo, n_rows * n_dev), BF16),
            jax.ShapeDtypeStruct((n_occ, wide), BF16),
            jax.ShapeDtypeStruct((n_occ, width), BF16),
        ],
        scratch_shapes=[pltpu.VMEM((n_occ, width), F32), pltpu.VMEM((n_occ, wide), BF16)],
        compiler_params=pltpu.CompilerParams(vmem_limit_bytes=16 * MIB),
        cost_estimate=pl.CostEstimate(flops=8 * n_occ * n_occ * n_mo, bytes_accessed=4 * MIB, transcendentals=0),
        name="rotation",
    )(*held, *other, hess, sel)
    sent = pl.pallas_call(
        functools.partial(half_kernel, n_rows, main),
        in_specs=[in_vmem] * 2,
        out_specs=in_vmem,
        out_shape=jax.ShapeDtypeStruct((n_dev, dest_rows, LANES), BF16),
        scratch_shapes=[
            pltpu.VMEM((q_loc * (r_loc - main), n_rows * n_dev), F32),
            pltpu.VMEM((q_loc, n_rows * n_dev, main), F32),
        ],
        compiler_params=pltpu.CompilerParams(vmem_limit_bytes=40 * MIB),
        cost_estimate=pl.CostEstimate(
            flops=2 * q_loc * r_loc * n_rows * n_dev * n_mo, bytes_accessed=2 * q_loc * r_loc * n_mo, transcendentals=0),
        name="half_rotation",
    )(chosen, three_vmem)

    got = lax.all_to_all(sent, BOTH, 0, 0, tiled=True).reshape(n_aux, n_orb, dest_rows, LANES)
    aux_step = min(n_aux, 8)
    out = pl.pallas_call(
        functools.partial(owner_kernel, n_rows, aux_step, q_loc, r_loc, main),
        grid=(n_aux // aux_step,),
        in_specs=[in_vmem] * 3,
        out_specs=pl.BlockSpec((aux_step * q_loc, n_rows * n_vir), lambda g: (g, 0)),
        out_shape=jax.ShapeDtypeStruct((n_aux * q_loc, n_rows * n_vir), BF16),
        compiler_params=pltpu.CompilerParams(vmem_limit_bytes=40 * MIB),
        cost_estimate=pl.CostEstimate(
            flops=4 * n_aux * q_loc * n_rows * n_occ * n_mo, bytes_accessed=8 * MIB, transcendentals=0),
        name="owner_rows",
    )(got, left, rot)
    if n_rows * n_vir != pairs:
        start = (lax.axis_index("aux") * pairs) % n_vir
        out = lax.dynamic_slice_in_dim(out, start, pairs, 1)
    return out[None]


def solution(mesh):
    def body(*args):
        return on_device(mesh.shape["aux"], mesh.shape["orb"], *args)

    return jax.shard_map(
        body,
        mesh=mesh,
        in_specs=(P("aux", "orb", None), P("aux", "orb", None), P()),
        out_specs=P("orb", None, "aux"),
        check_vma=False,
    )
```

```python
import functools
import math

import jax
import jax.numpy as jnp
import numpy as np
from jax import lax
from jax.experimental import pallas as pl
from jax.experimental.pallas import tpu as pltpu
from jax.sharding import PartitionSpec as P

BOTH = ("aux", "orb")
F32 = jnp.float32
BF16 = jnp.bfloat16
LANES = 128
MIB = 1 << 20


def matmul(a, b, dims):
    return lax.dot_general(a, b, (dims, ((), ())), preferred_element_type=F32)


NN = ((1,), (0,))
NT = ((1,), (1,))
TN = ((0,), (0,))


def to_hbm(x):
    return pltpu.with_memory_space_constraint(x, pltpu.HBM)


def my_index(n_orb):
    return lax.axis_index("aux") * n_orb + lax.axis_index("orb")


def swap(x, masks):
    return lax.ppermute(x, BOTH, [(d, d ^ mask) for d, mask in enumerate(masks)])


def tracks_of(n_dev):
    bits = n_dev.bit_length() - 1
    return [1, 2, *range(3, bits)], [2, 1, *range(bits - 1, 2, -1)]


def bit(index, which):
    return (index // (1 << which)) % 2


def half_of(index, n_dev):
    return sum(bit(index, k) for k in range(n_dev.bit_length() - 1)) % 2


def assemble(sources, width, rows):
    lane = lax.broadcasted_iota(jnp.int32, (rows, LANES), 1)
    rolled = {}

    def source_tile(which, tile, turn):
        key = (which, tile, turn)
        if key not in rolled:
            value = sources[which][0](tile)
            rolled[key] = pltpu.roll(value, turn, 1) if turn else value
        return rolled[key]

    tiles = []
    for start in range(0, width, LANES):
        result, end_done = None, 0
        for which, (_, src, dst, count) in enumerate(sources):
            low, high = max(dst, start), min(dst + count, start + LANES)
            turn = (dst - src) % LANES
            at = low
            while at < high:
                from_lane = at - dst + src
                tile = from_lane // LANES
                stop = min(high, at + LANES - from_lane % LANES)
                value = source_tile(which, tile, turn)
                if result is None:
                    result = value
                    if at > start:
                        result = jnp.where(lane >= at - start, value, 0.0)
                else:
                    result = jnp.where(lane >= at - start, value, result)
                end_done = stop - start
                at = stop
        if end_done < LANES:
            result = jnp.where(lane < end_done, result, 0.0)
        tiles.append(result)
    return tiles


def fock_half(side, lead, n_rows, base, ready, three_ref, dens_ref, part_refs, acc_ref):
    n_occ = dens_ref.shape[1]
    n_tiles = acc_ref.shape[0] // n_occ
    for static in (0, 1):

        @pl.when(side == static)
        def _(static=static):
            low = base + static * n_tiles * LANES
            high = min(three_ref.shape[2], low + n_tiles * LANES)
            for q in range(three_ref.shape[0]):
                ready(q)
                part = matmul(dens_ref[q], three_ref[q, :, low:high], NN)
                for t in range(n_tiles):
                    stop = min(LANES, high - low - t * LANES)
                    rows = slice(t * n_occ, (t + 1) * n_occ)
                    piece = part[:, t * LANES : t * LANES + stop]
                    if q:
                        acc_ref[rows, :stop] += piece
                    else:
                        if stop < LANES:
                            acc_ref[rows, :] = jnp.zeros((n_occ, LANES), F32)
                        acc_ref[rows, :stop] = piece

    for chain, ref in enumerate(part_refs):
        for j in (0, 1):
            start = pl.multiple_of((chain * 2 + (lead + j) % 2) * n_rows, n_rows)
            ref[j] = acc_ref[pl.ds(start, n_rows), :].astype(ref.dtype)


def side_and_lead(own, n_orb, n_dev, tracks):
    me = my_index(n_orb)
    side = half_of(me, n_dev) if own else 1 - half_of(me, n_dev)
    return side, jnp.where(side == 0, bit(me, tracks[0][0]), bit(me, tracks[1][0]))


def send_kernel(n_orb, n_dev, tracks, n_rows, base, three_hbm, dens_hbm,
                part_0, part_1, three_ref, dens_ref, acc_ref, sems, dens_sems):
    copies = []
    for q in range(three_ref.shape[0]):
        copies.append((
            pltpu.make_async_copy(dens_hbm.at[q], dens_ref.at[q], dens_sems.at[q]),
            pltpu.make_async_copy(three_hbm.at[q], three_ref.at[q], sems.at[q]),
        ))
        for copy in copies[q]:
            copy.start()

    def ready(q):
        for copy in copies[q]:
            copy.wait()

    side, lead = side_and_lead(False, n_orb, n_dev, tracks)
    fock_half(side, lead, n_rows, base, ready, three_ref, dens_ref, (part_0, part_1), acc_ref)


def keep_kernel(n_orb, n_dev, tracks, n_rows, base, three_ref, dens_ref, part_0, part_1, acc_ref):
    side, lead = side_and_lead(True, n_orb, n_dev, tracks)
    fock_half(side, lead, n_rows, base, lambda q: None, three_ref, dens_ref, (part_0, part_1), acc_ref)


def rotation_kernel(n_orb, n_dev, tracks, mine_0, mine_1, other_0, other_1, hess_ref, sel_ref, chosen_ref, left_ref, rot_ref, fock_ref, u_ref):
    n_occ, width = fock_ref.shape
    base = n_occ // LANES * LANES
    n_mo = chosen_ref.shape[0]
    mine_refs, other_refs = (mine_0, mine_1), (other_0, other_1)
    n_rows = mine_0.shape[1]
    step = math.gcd(n_rows, n_occ)
    me = my_index(n_orb)
    mine = half_of(me, n_dev)
    for start in range(0, 8 * n_rows, step):
        tile, row = divmod(start, n_occ)
        piece, at = divmod(start, n_rows)
        side, chain, j = piece // 4, piece // 2 % 2, piece % 2
        place = (j + bit(me, tracks[side][0])) % 2
        rows = slice(at, at + step)
        fock_ref[row : row + step, tile * LANES : (tile + 1) * LANES] = jnp.where(
            mine == side, mine_refs[chain][place, rows, :].astype(F32), other_refs[chain][place, rows, :].astype(F32))
    gen = -fock_ref[...] / hess_ref[...]
    square = jnp.sum(jnp.sum(gen * gen, axis=0, keepdims=True), axis=1, keepdims=True)
    rot = gen * jnp.minimum(1.0, math.sqrt(n_occ) / jnp.sqrt(square))
    rot_b = rot.astype(BF16)
    rot_ref[...] = rot_b
    over = matmul(rot_b, rot_b, NT)
    over_b = over.astype(BF16)
    over2 = matmul(over_b, over_b, NN)
    over_rot = matmul(over_b, rot_b, NN)
    eye = jnp.where(
        lax.broadcasted_iota(jnp.int32, (n_occ, n_occ), 0) == lax.broadcasted_iota(jnp.int32, (n_occ, n_occ), 1),
        1.0, 0.0)
    u_oo = (eye - over / 2.0 + over2 / 24.0).astype(BF16)
    u_ref[:, :base] = u_oo[:, :base]
    u_ref[:, base:] = (rot - over_rot / 6.0).astype(BF16)
    u_ref[:, base:n_occ] = u_oo[:, base:]
    l_oo = (over / 6.0 - eye).astype(BF16)
    left_ref[:, :base] = l_oo[:, :base]
    left_ref[:, base:] = (over_rot / 24.0 - rot / 2.0).astype(BF16)
    left_ref[:, base:n_occ] = l_oo[:, base:]
    chosen = matmul(u_ref[...], sel_ref[...], ((0,), (1,)))
    chosen_ref[...] = chosen[:n_mo].astype(BF16)


def swap_rows(tiles):
    row = lax.broadcasted_iota(jnp.int32, tiles[0].shape, 0)
    for step in (1, 2, 4):
        low = (row // step) % 2 == 0
        after = list(tiles)
        for t in range(8):
            if t & step == 0:
                first, second = tiles[t], tiles[t | step]
                after[t] = jnp.where(low, first, pltpu.roll(second, step, 0))
                after[t | step] = jnp.where(low, pltpu.roll(first, 8 - step, 0), second)
        tiles = after
    return tiles


def half_kernel(n_rows, main, chosen_ref, three_ref, sent_ref, rem_ref, half_ref):
    q_loc, r_loc, n_mo = three_ref.shape
    rem = r_loc - main
    n_dev, dest_rows = sent_ref.shape[:2]
    for q in range(q_loc):
        product = matmul(three_ref[q], chosen_ref[...], NN)
        half_ref[q] = product[:main].T
        rem_ref[q * rem : (q + 1) * rem, :] = product[main:]
    turned = rem_ref[...].T

    def group(at, dest):
        tile, k = divmod(at, n_rows)
        if tile < main // LANES:
            rows = slice(k * n_dev + dest, k * n_dev + dest + 8)
            return swap_rows([half_ref[q, rows, tile * LANES : (tile + 1) * LANES] for q in range(q_loc)])
        zero = jnp.zeros((8, LANES), F32)
        if at > main // LANES * n_rows:
            return [zero] * 8
        rest = [turned[k * n_dev + dest : k * n_dev + dest + 8, :] for k in range(n_rows)]
        return swap_rows(rest + [zero] * (8 - n_rows))

    for dest in range(0, n_dev, 8):
        for at in range(0, dest_rows // 8, 2):
            for d, pair in enumerate(zip(group(at, dest), group(at + 1, dest))):
                sent_ref[dest + d, at * 8 : at * 8 + 16, :] = jnp.concatenate(pair, 0).astype(BF16)


def owner_kernel(n_rows, n_aux, q_loc, r_loc, main, got_ref, left_ref, rot_ref, out_ref):
    n_orb = got_ref.shape[1]
    places = pl.ds(pl.program_id(0) * n_aux, n_aux)
    n_occ, wide = left_ref.shape
    width = rot_ref.shape[1]
    base = wide - width
    n_mo = n_orb * r_loc
    n_vir = n_mo - n_occ
    rem = r_loc - main
    group = n_rows * q_loc
    rows = n_aux * group
    lane_q = lax.broadcasted_iota(jnp.int32, (n_aux, q_loc, LANES), 2) // rem
    own_q = lane_q == lax.broadcasted_iota(jnp.int32, (n_aux, q_loc, LANES), 1)
    e_row = lax.broadcasted_iota(jnp.int32, (LANES, LANES), 0) % rem
    e_col = lax.broadcasted_iota(jnp.int32, (LANES, LANES), 1)

    sources = []
    rest = jnp.zeros((rows, LANES), F32)
    for b in range(n_orb):
        block = got_ref[places, b, :, :].astype(F32)
        pieces = [block[:, c * group : (c + 1) * group, :].reshape(rows, LANES) for c in range(main // LANES)]
        last = main // LANES * group
        spread = [
            jnp.where(own_q, jnp.broadcast_to(block[:, last + k : last + k + 1, :], own_q.shape), 0.0)
            for k in range(n_rows)
        ]
        spread = jnp.concatenate(spread, 1).reshape(rows, LANES).astype(BF16)
        rest = rest + matmul(spread, jnp.where(e_row + b * rem == e_col, 1.0, 0.0).astype(BF16), NN)
        sources.append((lambda tile, pieces=pieces: pieces[tile], 0, b * r_loc, main))
    for b in range(n_orb):
        sources.append((lambda tile: rest, b * rem, b * r_loc + main, rem))
    sources.sort(key=lambda entry: entry[2])
    half = jnp.concatenate(assemble(sources, wide, rows), 1)
    inner = matmul(half.astype(BF16), left_ref[...], NT).astype(BF16)
    total = half[:, base:] + matmul(inner, rot_ref[...], NN)
    total = total.reshape(n_aux, group, width)
    per_row = [total[:, k * q_loc : (k + 1) * q_loc, :].reshape(n_aux * q_loc, width) for k in range(n_rows)]
    sources = [
        (lambda tile, value=value: value[:, tile * LANES : (tile + 1) * LANES], n_occ - base, k * n_vir, n_vir)
        for k, value in enumerate(per_row)
    ]
    length = n_rows * n_vir
    for at, value in enumerate(assemble(sources, length, n_aux * q_loc)):
        stop = min(length, (at + 1) * LANES)
        out_ref[:, at * LANES : stop] = value[:, : stop - at * LANES].astype(BF16)


def on_device(n_aux, n_orb, three_index, density, hess_diag):
    n_dev = n_aux * n_orb
    q_loc, r_loc, n_mo = three_index.shape
    n_occ = density.shape[2]
    n_vir = n_mo - n_occ
    occ_blk = n_occ // n_orb
    pairs = occ_blk * n_vir // n_aux
    base = n_occ // LANES * LANES
    tiles = -(-(n_mo - base) // LANES)
    width = tiles * LANES
    main = r_loc // LANES * LANES
    assert n_dev & (n_dev - 1) == 0 and n_dev >= 8 and tiles % 4 == 0
    tracks = tracks_of(n_dev)
    whole = lambda *shape: pl.BlockSpec(shape, lambda *_: (0,) * len(shape))
    in_vmem = pl.BlockSpec(memory_space=pltpu.VMEM)

    half_shape = (2, tiles * n_occ // 8, LANES)
    in_hbm = pl.BlockSpec(memory_space=pltpu.HBM)
    piece_rows = tiles * n_occ // 8
    acc = pltpu.VMEM((tiles // 2 * n_occ, LANES), F32)
    cost = lambda moved: pl.CostEstimate(
        flops=q_loc * r_loc * n_occ * n_mo, bytes_accessed=moved, transcendentals=0)
    dens = density.transpose(0, 2, 1)
    *send, three_vmem, dens_vmem = pl.pallas_call(
        functools.partial(send_kernel, n_orb, n_dev, tracks, piece_rows, base),
        in_specs=[in_hbm] * 2,
        out_specs=[in_vmem] * 4,
        out_shape=[
            jax.ShapeDtypeStruct(half_shape, BF16),
            jax.ShapeDtypeStruct(half_shape, BF16),
            jax.ShapeDtypeStruct(three_index.shape, BF16),
            jax.ShapeDtypeStruct(dens.shape, BF16),
        ],
        scratch_shapes=[acc, pltpu.SemaphoreType.DMA((q_loc,)), pltpu.SemaphoreType.DMA((q_loc,))],
        compiler_params=pltpu.CompilerParams(vmem_limit_bytes=32 * MIB),
        cost_estimate=cost(2 * q_loc * r_loc * n_mo),
        name="fock_sent",
    )(to_hbm(three_index), to_hbm(dens))
    three_vmem = pltpu.with_memory_space_constraint(three_vmem, pltpu.VMEM)
    keep = pl.pallas_call(
        functools.partial(keep_kernel, n_orb, n_dev, tracks, piece_rows, base),
        in_specs=[in_vmem] * 2,
        out_specs=[in_vmem] * 2,
        out_shape=[jax.ShapeDtypeStruct(half_shape, F32)] * 2,
        scratch_shapes=[acc],
        compiler_params=pltpu.CompilerParams(vmem_limit_bytes=16 * MIB),
        cost_estimate=cost(MIB),
        name="fock_kept",
    )(three_vmem, pltpu.with_memory_space_constraint(dens_vmem, pltpu.VMEM))
    hess = jnp.pad(
        hess_diag.T, ((0, 0), (n_occ - base, width - (n_mo - base))), constant_values=jnp.inf)

    masks = [[1 | 1 << tracks[half_of(d, n_dev)][k] for d in range(n_dev)] for k in range(len(tracks[0]))]
    held, other = [], []
    for chain in (0, 1):
        part = keep[chain] + swap(send[chain], [1] * n_dev).astype(F32)
        piece = part[0] + swap(part[1].astype(BF16), masks[0]).astype(F32)
        for mask in masks[1:]:
            piece = piece + swap(piece.astype(BF16), mask).astype(F32)
        piece = piece.astype(BF16)
        held.append(jnp.stack([piece, swap(piece, masks[0])]))
        other.append(swap(held[chain], [1] * n_dev))

    assert q_loc == 8
    first = [p * pairs // n_vir for p in range(n_aux)]
    n_rows = max(-(-(p + 1) * pairs // n_vir) - first[p] for p in range(n_aux))
    sel = np.zeros((n_rows, n_aux, n_orb, n_occ), np.float32)
    for k in range(n_rows):
        for p in range(n_aux):
            for b in range(n_orb):
                sel[k, p, b, b * occ_blk + min(first[p] + k, occ_blk - 1)] = 1.0
    sel = jnp.asarray(sel.reshape(n_rows * n_dev, n_occ), BF16)

    dest_rows = -(-(main // LANES * n_rows * q_loc + n_rows) // 16) * 16
    wide = base + width
    chosen, left, rot = pl.pallas_call(
        functools.partial(rotation_kernel, n_orb, n_dev, tracks),
        in_specs=[in_vmem] * 6,
        out_specs=[in_vmem] * 3,
        out_shape=[
            jax.ShapeDtypeStruct((n_mo, n_rows * n_dev), BF16),
            jax.ShapeDtypeStruct((n_occ, wide), BF16),
            jax.ShapeDtypeStruct((n_occ, width), BF16),
        ],
        scratch_shapes=[pltpu.VMEM((n_occ, width), F32), pltpu.VMEM((n_occ, wide), BF16)],
        compiler_params=pltpu.CompilerParams(vmem_limit_bytes=16 * MIB),
        cost_estimate=pl.CostEstimate(flops=8 * n_occ * n_occ * n_mo, bytes_accessed=4 * MIB, transcendentals=0),
        name="rotation",
    )(*held, *other, hess, sel)
    sent = pl.pallas_call(
        functools.partial(half_kernel, n_rows, main),
        in_specs=[in_vmem] * 2,
        out_specs=in_vmem,
        out_shape=jax.ShapeDtypeStruct((n_dev, dest_rows, LANES), BF16),
        scratch_shapes=[
            pltpu.VMEM((q_loc * (r_loc - main), n_rows * n_dev), F32),
            pltpu.VMEM((q_loc, n_rows * n_dev, main), F32),
        ],
        compiler_params=pltpu.CompilerParams(vmem_limit_bytes=40 * MIB),
        cost_estimate=pl.CostEstimate(
            flops=2 * q_loc * r_loc * n_rows * n_dev * n_mo, bytes_accessed=2 * q_loc * r_loc * n_mo, transcendentals=0),
        name="half_rotation",
    )(chosen, three_vmem)

    got = lax.all_to_all(sent, BOTH, 0, 0, tiled=True).reshape(n_aux, n_orb, dest_rows, LANES)
    aux_step = min(n_aux, 8)
    out = pl.pallas_call(
        functools.partial(owner_kernel, n_rows, aux_step, q_loc, r_loc, main),
        grid=(n_aux // aux_step,),
        in_specs=[in_vmem] * 3,
        out_specs=pl.BlockSpec((aux_step * q_loc, n_rows * n_vir), lambda g: (g, 0)),
        out_shape=jax.ShapeDtypeStruct((n_aux * q_loc, n_rows * n_vir), BF16),
        compiler_params=pltpu.CompilerParams(vmem_limit_bytes=40 * MIB),
        cost_estimate=pl.CostEstimate(
            flops=4 * n_aux * q_loc * n_rows * n_occ * n_mo, bytes_accessed=8 * MIB, transcendentals=0),
        name="owner_rows",
    )(got, left, rot)
    if n_rows * n_vir != pairs:
        start = (lax.axis_index("aux") * pairs) % n_vir
        out = lax.dynamic_slice_in_dim(out, start, pairs, 1)
    return out[None]


def solution(mesh):
    def body(*args):
        return on_device(mesh.shape["aux"], mesh.shape["orb"], *args)

    return jax.shard_map(
        body,
        mesh=mesh,
        in_specs=(P("aux", "orb", None), P("aux", "orb", None), P()),
        out_specs=P("orb", None, "aux"),
        check_vma=False,
    )
```

```python
import functools
import math

import jax
import jax.numpy as jnp
import numpy as np
from jax import lax
from jax.experimental import pallas as pl
from jax.experimental.pallas import tpu as pltpu
from jax.sharding import PartitionSpec as P

BOTH = ("aux", "orb")
F32 = jnp.float32
BF16 = jnp.bfloat16
LANES = 128
MIB = 1 << 20


def matmul(a, b, dims):
    return lax.dot_general(a, b, (dims, ((), ())), preferred_element_type=F32)


NN = ((1,), (0,))
NT = ((1,), (1,))
TN = ((0,), (0,))


def to_hbm(x):
    return pltpu.with_memory_space_constraint(x, pltpu.HBM)


def my_index(n_orb):
    return lax.axis_index("aux") * n_orb + lax.axis_index("orb")


def swap(x, masks):
    return lax.ppermute(x, BOTH, [(d, d ^ mask) for d, mask in enumerate(masks)])


def tracks_of(n_dev):
    bits = n_dev.bit_length() - 1
    return [1, 2, *range(3, bits)], [2, 1, *range(bits - 1, 2, -1)]


def bit(index, which):
    return (index // (1 << which)) % 2


def half_of(index, n_dev):
    return sum(bit(index, k) for k in range(n_dev.bit_length() - 1)) % 2


def assemble(sources, width, rows):
    lane = lax.broadcasted_iota(jnp.int32, (rows, LANES), 1)
    rolled = {}

    def source_tile(which, tile, turn):
        key = (which, tile, turn)
        if key not in rolled:
            value = sources[which][0](tile)
            rolled[key] = pltpu.roll(value, turn, 1) if turn else value
        return rolled[key]

    tiles = []
    for start in range(0, width, LANES):
        result, end_done = None, 0
        for which, (_, src, dst, count) in enumerate(sources):
            low, high = max(dst, start), min(dst + count, start + LANES)
            turn = (dst - src) % LANES
            at = low
            while at < high:
                from_lane = at - dst + src
                tile = from_lane // LANES
                stop = min(high, at + LANES - from_lane % LANES)
                value = source_tile(which, tile, turn)
                if result is None:
                    result = value
                    if at > start:
                        result = jnp.where(lane >= at - start, value, 0.0)
                else:
                    result = jnp.where(lane >= at - start, value, result)
                end_done = stop - start
                at = stop
        if end_done < LANES:
            result = jnp.where(lane < end_done, result, 0.0)
        tiles.append(result)
    return tiles


def fock_kernel(n_orb, n_dev, tracks, three_hbm, dens_hbm, *refs):
    *part_refs, three_ref, acc_ref, dens_ref, sems, dens_sems = refs
    q_loc, _, n_mo = three_ref.shape
    n_occ = dens_ref.shape[1]
    n_tiles = acc_ref.shape[0] // n_occ
    base = n_occ // LANES * LANES
    copies = []
    for q in range(q_loc):
        copies.append((
            pltpu.make_async_copy(dens_hbm.at[q], dens_ref.at[q], dens_sems.at[q]),
            pltpu.make_async_copy(three_hbm.at[q], three_ref.at[q], sems.at[q]),
        ))
        for copy in copies[q]:
            copy.start()
    for q in range(q_loc):
        for copy in copies[q]:
            copy.wait()
        part = matmul(dens_ref[q], three_ref[q, :, base:], NN)
        for t in range(n_tiles):
            stop = min(LANES, n_mo - base - t * LANES)
            rows = slice(t * n_occ, (t + 1) * n_occ)
            piece = part[:, t * LANES : t * LANES + stop]
            if q:
                acc_ref[rows, :stop] += piece
            else:
                if stop < LANES:
                    acc_ref[rows, :] = jnp.zeros((n_occ, LANES), F32)
                acc_ref[rows, :stop] = piece
    me = my_index(n_orb)
    mine = half_of(me, n_dev)
    chains = len(part_refs) // 2
    n_rows = n_tiles * n_occ // (4 * chains)
    for chain in range(chains):
        for ref, side in zip(part_refs[chain::chains], (mine, 1 - mine)):
            lead = jnp.where(side == 0, bit(me, tracks[0][0]), bit(me, tracks[1][0]))
            for j in (0, 1):
                start = pl.multiple_of(((side * chains + chain) * 2 + (lead + j) % 2) * n_rows, n_rows)
                ref[j] = acc_ref[pl.ds(start, n_rows), :].astype(ref.dtype)


def rotation_kernel(n_orb, n_dev, tracks, *refs):
    *held_refs, hess_ref, sel_ref, chosen_ref, left_ref, rot_ref, fock_ref, u_ref = refs
    chains = len(held_refs) // 2
    mine_refs, other_refs = held_refs[:chains], held_refs[chains:]
    n_occ, width = fock_ref.shape
    base = n_occ // LANES * LANES
    n_mo = chosen_ref.shape[0]
    n_rows = mine_refs[0].shape[1]
    step = math.gcd(n_rows, n_occ)
    me = my_index(n_orb)
    mine = half_of(me, n_dev)
    for start in range(0, 4 * chains * n_rows, step):
        tile, row = divmod(start, n_occ)
        piece, at = divmod(start, n_rows)
        side, chain, j = piece // (2 * chains), piece // 2 % chains, piece % 2
        place = (j + bit(me, tracks[side][0])) % 2
        rows = slice(at, at + step)
        fock_ref[row : row + step, tile * LANES : (tile + 1) * LANES] = jnp.where(
            mine == side, mine_refs[chain][place, rows, :].astype(F32), other_refs[chain][place, rows, :].astype(F32))
    gen = -fock_ref[...] / hess_ref[...]
    square = jnp.sum(jnp.sum(gen * gen, axis=0, keepdims=True), axis=1, keepdims=True)
    rot = gen * jnp.minimum(1.0, math.sqrt(n_occ) / jnp.sqrt(square))
    rot_b = rot.astype(BF16)
    rot_ref[...] = rot_b
    over = matmul(rot_b, rot_b, NT)
    over_b = over.astype(BF16)
    over2 = matmul(over_b, over_b, NN)
    over_rot = matmul(over_b, rot_b, NN)
    eye = jnp.where(
        lax.broadcasted_iota(jnp.int32, (n_occ, n_occ), 0) == lax.broadcasted_iota(jnp.int32, (n_occ, n_occ), 1),
        1.0, 0.0)
    u_oo = (eye - over / 2.0 + over2 / 24.0).astype(BF16)
    u_ref[:, :base] = u_oo[:, :base]
    u_ref[:, base:] = (rot - over_rot / 6.0).astype(BF16)
    u_ref[:, base:n_occ] = u_oo[:, base:]
    l_oo = (over / 6.0 - eye).astype(BF16)
    left_ref[:, :base] = l_oo[:, :base]
    left_ref[:, base:] = (over_rot / 24.0 - rot / 2.0).astype(BF16)
    left_ref[:, base:n_occ] = l_oo[:, base:]
    chosen = matmul(sel_ref[...], u_ref[...], NN)
    chosen_ref[...] = chosen.T[:n_mo].astype(BF16)


def swap_rows(tiles):
    row = lax.broadcasted_iota(jnp.int32, tiles[0].shape, 0)
    for step in (1, 2, 4):
        low = (row // step) % 2 == 0
        after = list(tiles)
        for t in range(8):
            if t & step == 0:
                first, second = tiles[t], tiles[t | step]
                after[t] = jnp.where(low, first, pltpu.roll(second, step, 0))
                after[t | step] = jnp.where(low, pltpu.roll(first, 8 - step, 0), second)
        tiles = after
    return tiles


def half_kernel(n_rows, main, chosen_ref, three_ref, sent_ref, rem_ref, half_ref):
    q_loc, r_loc, n_mo = three_ref.shape
    rem = r_loc - main
    n_dev, dest_rows = sent_ref.shape[:2]
    for q in range(q_loc):
        product = matmul(three_ref[q], chosen_ref[...], NN)
        half_ref[q] = product[:main].T
        rem_ref[q * rem : (q + 1) * rem, :] = product[main:]
    turned = rem_ref[...].T

    def group(at, dest):
        tile, k = divmod(at, n_rows)
        if tile < main // LANES:
            rows = slice(k * n_dev + dest, k * n_dev + dest + 8)
            return swap_rows([half_ref[q, rows, tile * LANES : (tile + 1) * LANES] for q in range(q_loc)])
        zero = jnp.zeros((8, LANES), F32)
        if at > main // LANES * n_rows:
            return [zero] * 8
        rest = [turned[k * n_dev + dest : k * n_dev + dest + 8, :] for k in range(n_rows)]
        return swap_rows(rest + [zero] * (8 - n_rows))

    for dest in range(0, n_dev, 8):
        for at in range(0, dest_rows // 8, 2):
            for d, pair in enumerate(zip(group(at, dest), group(at + 1, dest))):
                sent_ref[dest + d, at * 8 : at * 8 + 16, :] = jnp.concatenate(pair, 0).astype(BF16)


def owner_kernel(n_rows, n_aux, q_loc, r_loc, main, got_ref, left_ref, rot_ref, out_ref):
    n_orb = got_ref.shape[1]
    places = pl.ds(pl.program_id(0) * n_aux, n_aux)
    n_occ, wide = left_ref.shape
    width = rot_ref.shape[1]
    base = wide - width
    n_mo = n_orb * r_loc
    n_vir = n_mo - n_occ
    rem = r_loc - main
    group = n_rows * q_loc
    rows = n_aux * group
    lane_q = lax.broadcasted_iota(jnp.int32, (n_aux, q_loc, LANES), 2) // rem
    own_q = lane_q == lax.broadcasted_iota(jnp.int32, (n_aux, q_loc, LANES), 1)
    e_row = lax.broadcasted_iota(jnp.int32, (LANES, LANES), 0) % rem
    e_col = lax.broadcasted_iota(jnp.int32, (LANES, LANES), 1)

    sources = []
    rest = jnp.zeros((rows, LANES), F32)
    for b in range(n_orb):
        block = got_ref[places, b, :, :].astype(F32)
        pieces = [block[:, c * group : (c + 1) * group, :].reshape(rows, LANES) for c in range(main // LANES)]
        last = main // LANES * group
        spread = [
            jnp.where(own_q, jnp.broadcast_to(block[:, last + k : last + k + 1, :], own_q.shape), 0.0)
            for k in range(n_rows)
        ]
        spread = jnp.concatenate(spread, 1).reshape(rows, LANES).astype(BF16)
        rest = rest + matmul(spread, jnp.where(e_row + b * rem == e_col, 1.0, 0.0).astype(BF16), NN)
        sources.append((lambda tile, pieces=pieces: pieces[tile], 0, b * r_loc, main))
    for b in range(n_orb):
        sources.append((lambda tile: rest, b * rem, b * r_loc + main, rem))
    sources.sort(key=lambda entry: entry[2])
    half = jnp.concatenate(assemble(sources, wide, rows), 1)
    inner = matmul(half.astype(BF16), left_ref[...], NT).astype(BF16)
    total = half[:, base:] + matmul(inner, rot_ref[...], NN)
    total = total.reshape(n_aux, group, width)
    per_row = [total[:, k * q_loc : (k + 1) * q_loc, :].reshape(n_aux * q_loc, width) for k in range(n_rows)]
    sources = [
        (lambda tile, value=value: value[:, tile * LANES : (tile + 1) * LANES], n_occ - base, k * n_vir, n_vir)
        for k, value in enumerate(per_row)
    ]
    length = n_rows * n_vir
    for at, value in enumerate(assemble(sources, length, n_aux * q_loc)):
        stop = min(length, (at + 1) * LANES)
        out_ref[:, at * LANES : stop] = value[:, : stop - at * LANES].astype(BF16)


def on_device(n_aux, n_orb, three_index, density, hess_diag):
    n_dev = n_aux * n_orb
    q_loc, r_loc, n_mo = three_index.shape
    n_occ = density.shape[2]
    n_vir = n_mo - n_occ
    occ_blk = n_occ // n_orb
    pairs = occ_blk * n_vir // n_aux
    base = n_occ // LANES * LANES
    tiles = -(-(n_mo - base) // LANES)
    width = tiles * LANES
    main = r_loc // LANES * LANES
    assert n_dev & (n_dev - 1) == 0 and n_dev >= 8 and tiles % 4 == 0
    tracks = tracks_of(n_dev)
    whole = lambda *shape: pl.BlockSpec(shape, lambda *_: (0,) * len(shape))
    in_vmem = pl.BlockSpec(memory_space=pltpu.VMEM)

    chains = 3
    half_shape = (2, tiles * n_occ // (4 * chains), LANES)
    in_hbm = pl.BlockSpec(memory_space=pltpu.HBM)
    *parts, three_vmem = pl.pallas_call(
        functools.partial(fock_kernel, n_orb, n_dev, tracks),
        in_specs=[in_hbm, in_hbm],
        out_specs=[in_vmem] * (2 * chains + 1),
        out_shape=[
            *[jax.ShapeDtypeStruct(half_shape, F32)] * chains,
            *[jax.ShapeDtypeStruct(half_shape, BF16)] * chains,
            jax.ShapeDtypeStruct(three_index.shape, BF16),
        ],
        scratch_shapes=[
            pltpu.VMEM((tiles * n_occ, LANES), F32),
            pltpu.VMEM((q_loc, n_occ, r_loc), BF16),
            pltpu.SemaphoreType.DMA((q_loc,)),
            pltpu.SemaphoreType.DMA((q_loc,)),
        ],
        compiler_params=pltpu.CompilerParams(vmem_limit_bytes=38 * MIB),
        cost_estimate=pl.CostEstimate(
            flops=2 * q_loc * r_loc * n_occ * n_mo, bytes_accessed=2 * q_loc * r_loc * n_mo, transcendentals=0),
        name="fock",
    )(to_hbm(three_index), to_hbm(density.transpose(0, 2, 1)))
    hess = jnp.pad(
        hess_diag.T, ((0, 0), (n_occ - base, width - (n_mo - base))), constant_values=jnp.inf)

    masks = [[1 | 1 << tracks[half_of(d, n_dev)][k] for d in range(n_dev)] for k in range(len(tracks[0]))]
    held, other = [], []
    for chain in range(chains):
        part = parts[chain] + swap(parts[chains + chain], [1] * n_dev).astype(F32)
        piece = part[0] + swap(part[1].astype(BF16), masks[0]).astype(F32)
        for mask in masks[1:]:
            piece = piece + swap(piece.astype(BF16), mask).astype(F32)
        piece = piece.astype(BF16)
        held.append(jnp.stack([piece, swap(piece, masks[0])]))
        other.append(swap(held[chain], [1] * n_dev))

    assert q_loc == 8
    first = [p * pairs // n_vir for p in range(n_aux)]
    n_rows = max(-(-(p + 1) * pairs // n_vir) - first[p] for p in range(n_aux))
    sel = np.zeros((n_rows, n_aux, n_orb, n_occ), np.float32)
    for k in range(n_rows):
        for p in range(n_aux):
            for b in range(n_orb):
                sel[k, p, b, b * occ_blk + min(first[p] + k, occ_blk - 1)] = 1.0
    sel = jnp.asarray(sel.reshape(n_rows * n_dev, n_occ), BF16)

    dest_rows = -(-(main // LANES * n_rows * q_loc + n_rows) // 16) * 16
    wide = base + width
    chosen, left, rot = pl.pallas_call(
        functools.partial(rotation_kernel, n_orb, n_dev, tracks),
        in_specs=[in_vmem] * (2 * chains + 2),
        out_specs=[in_vmem] * 3,
        out_shape=[
            jax.ShapeDtypeStruct((n_mo, n_rows * n_dev), BF16),
            jax.ShapeDtypeStruct((n_occ, wide), BF16),
            jax.ShapeDtypeStruct((n_occ, width), BF16),
        ],
        scratch_shapes=[pltpu.VMEM((n_occ, width), F32), pltpu.VMEM((n_occ, wide), BF16)],
        compiler_params=pltpu.CompilerParams(vmem_limit_bytes=16 * MIB),
        cost_estimate=pl.CostEstimate(flops=8 * n_occ * n_occ * n_mo, bytes_accessed=4 * MIB, transcendentals=0),
        name="rotation",
    )(*held, *other, hess, sel)
    sent = pl.pallas_call(
        functools.partial(half_kernel, n_rows, main),
        in_specs=[in_vmem] * 2,
        out_specs=in_vmem,
        out_shape=jax.ShapeDtypeStruct((n_dev, dest_rows, LANES), BF16),
        scratch_shapes=[
            pltpu.VMEM((q_loc * (r_loc - main), n_rows * n_dev), F32),
            pltpu.VMEM((q_loc, n_rows * n_dev, main), F32),
        ],
        compiler_params=pltpu.CompilerParams(vmem_limit_bytes=40 * MIB),
        cost_estimate=pl.CostEstimate(
            flops=2 * q_loc * r_loc * n_rows * n_dev * n_mo, bytes_accessed=2 * q_loc * r_loc * n_mo, transcendentals=0),
        name="half_rotation",
    )(chosen, three_vmem)

    got = lax.all_to_all(sent, BOTH, 0, 0, tiled=True).reshape(n_aux, n_orb, dest_rows, LANES)
    aux_step = min(n_aux, 8)
    out = pl.pallas_call(
        functools.partial(owner_kernel, n_rows, aux_step, q_loc, r_loc, main),
        grid=(n_aux // aux_step,),
        in_specs=[in_vmem] * 3,
        out_specs=pl.BlockSpec((aux_step * q_loc, n_rows * n_vir), lambda g: (g, 0)),
        out_shape=jax.ShapeDtypeStruct((n_aux * q_loc, n_rows * n_vir), BF16),
        compiler_params=pltpu.CompilerParams(vmem_limit_bytes=40 * MIB),
        cost_estimate=pl.CostEstimate(
            flops=4 * n_aux * q_loc * n_rows * n_occ * n_mo, bytes_accessed=8 * MIB, transcendentals=0),
        name="owner_rows",
    )(got, left, rot)
    if n_rows * n_vir != pairs:
        start = (lax.axis_index("aux") * pairs) % n_vir
        out = lax.dynamic_slice_in_dim(out, start, pairs, 1)
    return out[None]


def solution(mesh):
    def body(*args):
        return on_device(mesh.shape["aux"], mesh.shape["orb"], *args)

    return jax.shard_map(
        body,
        mesh=mesh,
        in_specs=(P("aux", "orb", None), P("aux", "orb", None), P()),
        out_specs=P("orb", None, "aux"),
        check_vma=False,
    )
```

```python
import functools
import math

import jax
import jax.numpy as jnp
import numpy as np
from jax import lax
from jax.experimental import pallas as pl
from jax.experimental.pallas import tpu as pltpu
from jax.sharding import PartitionSpec as P

BOTH = ("aux", "orb")
F32 = jnp.float32
BF16 = jnp.bfloat16
LANES = 128
MIB = 1 << 20


def matmul(a, b, dims):
    return lax.dot_general(a, b, (dims, ((), ())), preferred_element_type=F32)


NN = ((1,), (0,))
NT = ((1,), (1,))
TN = ((0,), (0,))


def to_hbm(x):
    return pltpu.with_memory_space_constraint(x, pltpu.HBM)


def my_index(n_orb):
    return lax.axis_index("aux") * n_orb + lax.axis_index("orb")


def swap(x, masks):
    return lax.ppermute(x, BOTH, [(d, d ^ mask) for d, mask in enumerate(masks)])


def tracks_of(n_dev):
    bits = n_dev.bit_length() - 1
    return [1, 2, *range(3, bits)], [2, 1, *range(bits - 1, 2, -1)]


def bit(index, which):
    return (index // (1 << which)) % 2


def half_of(index, n_dev):
    return sum(bit(index, k) for k in range(n_dev.bit_length() - 1)) % 2


def assemble(sources, width, rows):
    lane = lax.broadcasted_iota(jnp.int32, (rows, LANES), 1)
    rolled = {}

    def source_tile(which, tile, turn):
        key = (which, tile, turn)
        if key not in rolled:
            value = sources[which][0](tile)
            rolled[key] = pltpu.roll(value, turn, 1) if turn else value
        return rolled[key]

    tiles = []
    for start in range(0, width, LANES):
        result, end_done = None, 0
        for which, (_, src, dst, count) in enumerate(sources):
            low, high = max(dst, start), min(dst + count, start + LANES)
            turn = (dst - src) % LANES
            at = low
            while at < high:
                from_lane = at - dst + src
                tile = from_lane // LANES
                stop = min(high, at + LANES - from_lane % LANES)
                value = source_tile(which, tile, turn)
                if result is None:
                    result = value
                    if at > start:
                        result = jnp.where(lane >= at - start, value, 0.0)
                else:
                    result = jnp.where(lane >= at - start, value, result)
                end_done = stop - start
                at = stop
        if end_done < LANES:
            result = jnp.where(lane < end_done, result, 0.0)
        tiles.append(result)
    return tiles


def fock_kernel(n_orb, n_dev, tracks, three_hbm, dens_hbm, *refs):
    *part_refs, three_ref, acc_ref, dens_ref, sems, dens_sems = refs
    q_loc, _, n_mo = three_ref.shape
    n_occ = dens_ref.shape[1]
    n_tiles = acc_ref.shape[0] // n_occ
    base = n_occ // LANES * LANES
    copies = []
    for q in range(q_loc):
        copies.append((
            pltpu.make_async_copy(dens_hbm.at[q], dens_ref.at[q], dens_sems.at[q]),
            pltpu.make_async_copy(three_hbm.at[q], three_ref.at[q], sems.at[q]),
        ))
        for copy in copies[q]:
            copy.start()
    for q in range(q_loc):
        for copy in copies[q]:
            copy.wait()
        part = matmul(dens_ref[q], three_ref[q, :, base:], NN)
        for t in range(n_tiles):
            stop = min(LANES, n_mo - base - t * LANES)
            rows = slice(t * n_occ, (t + 1) * n_occ)
            piece = part[:, t * LANES : t * LANES + stop]
            if q:
                acc_ref[rows, :stop] += piece
            else:
                if stop < LANES:
                    acc_ref[rows, :] = jnp.zeros((n_occ, LANES), F32)
                acc_ref[rows, :stop] = piece
    me = my_index(n_orb)
    mine = half_of(me, n_dev)
    chains = len(part_refs) // 2
    n_rows = n_tiles * n_occ // (4 * chains)
    for chain in range(chains):
        for ref, side in zip(part_refs[chain::chains], (mine, 1 - mine)):
            lead = jnp.where(side == 0, bit(me, tracks[0][0]), bit(me, tracks[1][0]))
            for j in (0, 1):
                start = pl.multiple_of(((side * chains + chain) * 2 + (lead + j) % 2) * n_rows, n_rows)
                ref[j] = acc_ref[pl.ds(start, n_rows), :].astype(ref.dtype)


def swap_rows(tiles):
    row = lax.broadcasted_iota(jnp.int32, tiles[0].shape, 0)
    for step in (1, 2, 4):
        low = (row // step) % 2 == 0
        after = list(tiles)
        for t in range(8):
            if t & step == 0:
                first, second = tiles[t], tiles[t | step]
                after[t] = jnp.where(low, first, pltpu.roll(second, step, 0))
                after[t | step] = jnp.where(low, pltpu.roll(first, 8 - step, 0), second)
        tiles = after
    return tiles


def rotate_kernel(n_orb, n_dev, tracks, n_rows, main, *refs):
    *held_refs, hess_ref, sel_ref, three_ref, sent_ref, left_ref, rot_ref, fock_ref, u_ref, chosen_ref, rem_ref, half_ref = refs
    chains = len(held_refs) // 2
    mine_refs, other_refs = held_refs[:chains], held_refs[chains:]
    n_occ, width = fock_ref.shape
    base = n_occ // LANES * LANES
    n_mo = chosen_ref.shape[0]
    piece_rows = mine_refs[0].shape[1]
    step = math.gcd(piece_rows, n_occ)
    me = my_index(n_orb)
    mine = half_of(me, n_dev)
    for start in range(0, 4 * chains * piece_rows, step):
        tile, row = divmod(start, n_occ)
        piece, at = divmod(start, piece_rows)
        side, chain, j = piece // (2 * chains), piece // 2 % chains, piece % 2
        place = (j + bit(me, tracks[side][0])) % 2
        rows = slice(at, at + step)
        fock_ref[row : row + step, tile * LANES : (tile + 1) * LANES] = jnp.where(
            mine == side, mine_refs[chain][place, rows, :].astype(F32), other_refs[chain][place, rows, :].astype(F32))
    gen = -fock_ref[...] / hess_ref[...]
    square = jnp.sum(jnp.sum(gen * gen, axis=0, keepdims=True), axis=1, keepdims=True)
    rot = gen * jnp.minimum(1.0, math.sqrt(n_occ) / jnp.sqrt(square))
    rot_b = rot.astype(BF16)
    rot_ref[...] = rot_b
    over = matmul(rot_b, rot_b, NT)
    over_b = over.astype(BF16)
    over2 = matmul(over_b, over_b, NN)
    over_rot = matmul(over_b, rot_b, NN)
    eye = jnp.where(
        lax.broadcasted_iota(jnp.int32, (n_occ, n_occ), 0) == lax.broadcasted_iota(jnp.int32, (n_occ, n_occ), 1),
        1.0, 0.0)
    u_oo = (eye - over / 2.0 + over2 / 24.0).astype(BF16)
    u_ref[:, :base] = u_oo[:, :base]
    u_ref[:, base:] = (rot - over_rot / 6.0).astype(BF16)
    u_ref[:, base:n_occ] = u_oo[:, base:]
    chosen = matmul(sel_ref[...], u_ref[...], NN)
    chosen_ref[...] = chosen.T[:n_mo].astype(BF16)
    q_loc, r_loc, n_mo = three_ref.shape
    rem = r_loc - main
    n_dev, dest_rows = sent_ref.shape[:2]
    for q in range(q_loc):
        product = matmul(three_ref[q], chosen_ref[...], NN)
        half_ref[q] = product[:main].T
        rem_ref[q * rem : (q + 1) * rem, :] = product[main:]
    l_oo = (over / 6.0 - eye).astype(BF16)
    left_ref[:, :base] = l_oo[:, :base]
    left_ref[:, base:] = (over_rot / 24.0 - rot / 2.0).astype(BF16)
    left_ref[:, base:n_occ] = l_oo[:, base:]
    turned = rem_ref[...].T

    def group(at, dest):
        tile, k = divmod(at, n_rows)
        if tile < main // LANES:
            rows = slice(k * n_dev + dest, k * n_dev + dest + 8)
            return swap_rows([half_ref[q, rows, tile * LANES : (tile + 1) * LANES] for q in range(q_loc)])
        zero = jnp.zeros((8, LANES), F32)
        if at > main // LANES * n_rows:
            return [zero] * 8
        rest = [turned[k * n_dev + dest : k * n_dev + dest + 8, :] for k in range(n_rows)]
        return swap_rows(rest + [zero] * (8 - n_rows))

    for dest in range(0, n_dev, 8):
        for at in range(0, dest_rows // 8, 2):
            for d, pair in enumerate(zip(group(at, dest), group(at + 1, dest))):
                sent_ref[dest + d, at * 8 : at * 8 + 16, :] = jnp.concatenate(pair, 0).astype(BF16)


def owner_kernel(n_rows, n_aux, q_loc, r_loc, main, got_ref, left_ref, rot_ref, out_ref):
    n_orb = got_ref.shape[1]
    places = pl.ds(pl.program_id(0) * n_aux, n_aux)
    n_occ, wide = left_ref.shape
    width = rot_ref.shape[1]
    base = wide - width
    n_mo = n_orb * r_loc
    n_vir = n_mo - n_occ
    rem = r_loc - main
    group = n_rows * q_loc
    rows = n_aux * group
    lane_q = lax.broadcasted_iota(jnp.int32, (n_aux, q_loc, LANES), 2) // rem
    own_q = lane_q == lax.broadcasted_iota(jnp.int32, (n_aux, q_loc, LANES), 1)
    e_row = lax.broadcasted_iota(jnp.int32, (LANES, LANES), 0) % rem
    e_col = lax.broadcasted_iota(jnp.int32, (LANES, LANES), 1)

    sources = []
    rest = jnp.zeros((rows, LANES), F32)
    for b in range(n_orb):
        block = got_ref[places, b, :, :].astype(F32)
        pieces = [block[:, c * group : (c + 1) * group, :].reshape(rows, LANES) for c in range(main // LANES)]
        last = main // LANES * group
        spread = [
            jnp.where(own_q, jnp.broadcast_to(block[:, last + k : last + k + 1, :], own_q.shape), 0.0)
            for k in range(n_rows)
        ]
        spread = jnp.concatenate(spread, 1).reshape(rows, LANES).astype(BF16)
        rest = rest + matmul(spread, jnp.where(e_row + b * rem == e_col, 1.0, 0.0).astype(BF16), NN)
        sources.append((lambda tile, pieces=pieces: pieces[tile], 0, b * r_loc, main))
    for b in range(n_orb):
        sources.append((lambda tile: rest, b * rem, b * r_loc + main, rem))
    sources.sort(key=lambda entry: entry[2])
    half = jnp.concatenate(assemble(sources, wide, rows), 1)
    inner = matmul(half.astype(BF16), left_ref[...], NT).astype(BF16)
    total = half[:, base:] + matmul(inner, rot_ref[...], NN)
    total = total.reshape(n_aux, group, width)
    per_row = [total[:, k * q_loc : (k + 1) * q_loc, :].reshape(n_aux * q_loc, width) for k in range(n_rows)]
    sources = [
        (lambda tile, value=value: value[:, tile * LANES : (tile + 1) * LANES], n_occ - base, k * n_vir, n_vir)
        for k, value in enumerate(per_row)
    ]
    length = n_rows * n_vir
    for at, value in enumerate(assemble(sources, length, n_aux * q_loc)):
        stop = min(length, (at + 1) * LANES)
        out_ref[:, at * LANES : stop] = value[:, : stop - at * LANES].astype(BF16)


def on_device(n_aux, n_orb, three_index, density, hess_diag):
    n_dev = n_aux * n_orb
    q_loc, r_loc, n_mo = three_index.shape
    n_occ = density.shape[2]
    n_vir = n_mo - n_occ
    occ_blk = n_occ // n_orb
    pairs = occ_blk * n_vir // n_aux
    base = n_occ // LANES * LANES
    tiles = -(-(n_mo - base) // LANES)
    width = tiles * LANES
    main = r_loc // LANES * LANES
    assert n_dev & (n_dev - 1) == 0 and n_dev >= 8 and tiles % 4 == 0
    tracks = tracks_of(n_dev)
    whole = lambda *shape: pl.BlockSpec(shape, lambda *_: (0,) * len(shape))
    in_vmem = pl.BlockSpec(memory_space=pltpu.VMEM)

    chains = 3
    half_shape = (2, tiles * n_occ // (4 * chains), LANES)
    in_hbm = pl.BlockSpec(memory_space=pltpu.HBM)
    *parts, three_vmem = pl.pallas_call(
        functools.partial(fock_kernel, n_orb, n_dev, tracks),
        in_specs=[in_hbm, in_hbm],
        out_specs=[in_vmem] * (2 * chains + 1),
        out_shape=[
            *[jax.ShapeDtypeStruct(half_shape, F32)] * chains,
            *[jax.ShapeDtypeStruct(half_shape, BF16)] * chains,
            jax.ShapeDtypeStruct(three_index.shape, BF16),
        ],
        scratch_shapes=[
            pltpu.VMEM((tiles * n_occ, LANES), F32),
            pltpu.VMEM((q_loc, n_occ, r_loc), BF16),
            pltpu.SemaphoreType.DMA((q_loc,)),
            pltpu.SemaphoreType.DMA((q_loc,)),
        ],
        compiler_params=pltpu.CompilerParams(vmem_limit_bytes=38 * MIB),
        cost_estimate=pl.CostEstimate(
            flops=2 * q_loc * r_loc * n_occ * n_mo, bytes_accessed=2 * q_loc * r_loc * n_mo, transcendentals=0),
        name="fock",
    )(to_hbm(three_index), to_hbm(density.transpose(0, 2, 1)))
    hess = jnp.pad(
        hess_diag.T, ((0, 0), (n_occ - base, width - (n_mo - base))), constant_values=jnp.inf)

    masks = [[1 | 1 << tracks[half_of(d, n_dev)][k] for d in range(n_dev)] for k in range(len(tracks[0]))]
    held, other = [], []
    for chain in range(chains):
        part = parts[chain] + swap(parts[chains + chain], [1] * n_dev).astype(F32)
        piece = part[0] + swap(part[1].astype(BF16), masks[0]).astype(F32)
        for mask in masks[1:]:
            piece = piece + swap(piece.astype(BF16), mask).astype(F32)
        piece = piece.astype(BF16)
        held.append(jnp.stack([piece, swap(piece, masks[0])]))
        other.append(swap(held[chain], [1] * n_dev))

    assert q_loc == 8
    first = [p * pairs // n_vir for p in range(n_aux)]
    n_rows = max(-(-(p + 1) * pairs // n_vir) - first[p] for p in range(n_aux))
    sel = np.zeros((n_rows, n_aux, n_orb, n_occ), np.float32)
    for k in range(n_rows):
        for p in range(n_aux):
            for b in range(n_orb):
                sel[k, p, b, b * occ_blk + min(first[p] + k, occ_blk - 1)] = 1.0
    sel = jnp.asarray(sel.reshape(n_rows * n_dev, n_occ), BF16)

    dest_rows = -(-(main // LANES * n_rows * q_loc + n_rows) // 16) * 16
    wide = base + width
    sent, left, rot = pl.pallas_call(
        functools.partial(rotate_kernel, n_orb, n_dev, tracks, n_rows, main),
        in_specs=[in_vmem] * (2 * chains + 3),
        out_specs=[in_vmem] * 3,
        out_shape=[
            jax.ShapeDtypeStruct((n_dev, dest_rows, LANES), BF16),
            jax.ShapeDtypeStruct((n_occ, wide), BF16),
            jax.ShapeDtypeStruct((n_occ, width), BF16),
        ],
        scratch_shapes=[
            pltpu.VMEM((n_occ, width), F32),
            pltpu.VMEM((n_occ, wide), BF16),
            pltpu.VMEM((n_mo, n_rows * n_dev), BF16),
            pltpu.VMEM((q_loc * (r_loc - main), n_rows * n_dev), F32),
            pltpu.VMEM((q_loc, n_rows * n_dev, main), F32),
        ],
        compiler_params=pltpu.CompilerParams(vmem_limit_bytes=40 * MIB),
        cost_estimate=pl.CostEstimate(
            flops=2 * q_loc * r_loc * n_rows * n_dev * n_mo, bytes_accessed=2 * q_loc * r_loc * n_mo, transcendentals=0),
        name="half_rotation",
    )(*held, *other, hess, sel, three_vmem)

    got = lax.all_to_all(sent, BOTH, 0, 0, tiled=True).reshape(n_aux, n_orb, dest_rows, LANES)
    aux_step = min(n_aux, 8)
    out = pl.pallas_call(
        functools.partial(owner_kernel, n_rows, aux_step, q_loc, r_loc, main),
        grid=(n_aux // aux_step,),
        in_specs=[in_vmem] * 3,
        out_specs=pl.BlockSpec((aux_step * q_loc, n_rows * n_vir), lambda g: (g, 0)),
        out_shape=jax.ShapeDtypeStruct((n_aux * q_loc, n_rows * n_vir), BF16),
        compiler_params=pltpu.CompilerParams(vmem_limit_bytes=40 * MIB),
        cost_estimate=pl.CostEstimate(
            flops=4 * n_aux * q_loc * n_rows * n_occ * n_mo, bytes_accessed=8 * MIB, transcendentals=0),
        name="owner_rows",
    )(got, left, rot)
    if n_rows * n_vir != pairs:
        start = (lax.axis_index("aux") * pairs) % n_vir
        out = lax.dynamic_slice_in_dim(out, start, pairs, 1)
    return out[None]


def solution(mesh):
    def body(*args):
        return on_device(mesh.shape["aux"], mesh.shape["orb"], *args)

    return jax.shard_map(
        body,
        mesh=mesh,
        in_specs=(P("aux", "orb", None), P("aux", "orb", None), P()),
        out_specs=P("orb", None, "aux"),
        check_vma=False,
    )
```

```python
import functools
import math

import jax
import jax.numpy as jnp
import numpy as np
from jax import lax
from jax.experimental import pallas as pl
from jax.experimental.pallas import tpu as pltpu
from jax.sharding import PartitionSpec as P

BOTH = ("aux", "orb")
F32 = jnp.float32
BF16 = jnp.bfloat16
LANES = 128
MIB = 1 << 20


def matmul(a, b, dims):
    return lax.dot_general(a, b, (dims, ((), ())), preferred_element_type=F32)


NN = ((1,), (0,))
NT = ((1,), (1,))
TN = ((0,), (0,))


def to_hbm(x):
    return pltpu.with_memory_space_constraint(x, pltpu.HBM)


def my_index(n_orb):
    return lax.axis_index("aux") * n_orb + lax.axis_index("orb")


def swap(x, masks):
    return lax.ppermute(x, BOTH, [(d, d ^ mask) for d, mask in enumerate(masks)])


def tracks_of(n_dev):
    bits = n_dev.bit_length() - 1
    return [1, 2, *range(3, bits)], [2, 1, *range(bits - 1, 2, -1)]


def bit(index, which):
    return (index // (1 << which)) % 2


def half_of(index, n_dev):
    return sum(bit(index, k) for k in range(n_dev.bit_length() - 1)) % 2


def assemble(sources, width, rows):
    lane = lax.broadcasted_iota(jnp.int32, (rows, LANES), 1)
    rolled = {}

    def source_tile(which, tile, turn):
        key = (which, tile, turn)
        if key not in rolled:
            value = sources[which][0](tile)
            rolled[key] = pltpu.roll(value, turn, 1) if turn else value
        return rolled[key]

    tiles = []
    for start in range(0, width, LANES):
        result, end_done = None, 0
        for which, (_, src, dst, count) in enumerate(sources):
            low, high = max(dst, start), min(dst + count, start + LANES)
            turn = (dst - src) % LANES
            at = low
            while at < high:
                from_lane = at - dst + src
                tile = from_lane // LANES
                stop = min(high, at + LANES - from_lane % LANES)
                value = source_tile(which, tile, turn)
                if result is None:
                    result = value
                    if at > start:
                        result = jnp.where(lane >= at - start, value, 0.0)
                else:
                    result = jnp.where(lane >= at - start, value, result)
                end_done = stop - start
                at = stop
        if end_done < LANES:
            result = jnp.where(lane < end_done, result, 0.0)
        tiles.append(result)
    return tiles


def fock_kernel(n_orb, n_dev, tracks, three_hbm, dens_hbm, *refs):
    *part_refs, three_ref, acc_ref, dens_ref, sems, dens_sems = refs
    q_loc, _, n_mo = three_ref.shape
    n_occ = dens_ref.shape[1]
    n_tiles = acc_ref.shape[0] // n_occ
    base = n_occ // LANES * LANES
    copies = []
    for q in range(q_loc):
        copies.append((
            pltpu.make_async_copy(dens_hbm.at[q], dens_ref.at[q], dens_sems.at[q]),
            pltpu.make_async_copy(three_hbm.at[q], three_ref.at[q], sems.at[q]),
        ))
        for copy in copies[q]:
            copy.start()
    for q in range(q_loc):
        for copy in copies[q]:
            copy.wait()
        part = matmul(dens_ref[q], three_ref[q, :, base:], NN)
        for t in range(n_tiles):
            stop = min(LANES, n_mo - base - t * LANES)
            rows = slice(t * n_occ, (t + 1) * n_occ)
            piece = part[:, t * LANES : t * LANES + stop]
            if q:
                acc_ref[rows, :stop] += piece
            else:
                if stop < LANES:
                    acc_ref[rows, :] = jnp.zeros((n_occ, LANES), F32)
                acc_ref[rows, :stop] = piece
    me = my_index(n_orb)
    mine = half_of(me, n_dev)
    chains = len(part_refs) // 2
    n_rows = n_tiles * n_occ // (4 * chains)
    for chain in range(chains):
        for ref, side in zip(part_refs[chain::chains], (mine, 1 - mine)):
            lead = jnp.where(side == 0, bit(me, tracks[0][0]), bit(me, tracks[1][0]))
            for j in (0, 1):
                start = pl.multiple_of(((side * chains + chain) * 2 + (lead + j) % 2) * n_rows, n_rows)
                ref[j] = acc_ref[pl.ds(start, n_rows), :].astype(ref.dtype)


def swap_rows(tiles):
    row = lax.broadcasted_iota(jnp.int32, tiles[0].shape, 0)
    for step in (1, 2, 4):
        low = (row // step) % 2 == 0
        after = list(tiles)
        for t in range(8):
            if t & step == 0:
                first, second = tiles[t], tiles[t | step]
                after[t] = jnp.where(low, first, pltpu.roll(second, step, 0))
                after[t | step] = jnp.where(low, pltpu.roll(first, 8 - step, 0), second)
        tiles = after
    return tiles


def rotate_kernel(n_orb, n_dev, tracks, n_rows, main, *refs):
    *held_refs, hess_ref, sel_ref, three_ref, sent_ref, left_ref, rot_ref, fock_ref, u_ref, chosen_ref, rem_ref, half_ref = refs
    chains = len(held_refs) // 2
    mine_refs, other_refs = held_refs[:chains], held_refs[chains:]
    n_occ, width = fock_ref.shape
    base = n_occ // LANES * LANES
    n_mo = chosen_ref.shape[0]
    piece_rows = mine_refs[0].shape[1]
    step = math.gcd(piece_rows, n_occ)
    me = my_index(n_orb)
    mine = half_of(me, n_dev)
    for start in range(0, 4 * chains * piece_rows, step):
        tile, row = divmod(start, n_occ)
        piece, at = divmod(start, piece_rows)
        side, chain, j = piece // (2 * chains), piece // 2 % chains, piece % 2
        place = (j + bit(me, tracks[side][0])) % 2
        rows = slice(at, at + step)
        fock_ref[row : row + step, tile * LANES : (tile + 1) * LANES] = jnp.where(
            mine == side, mine_refs[chain][place, rows, :].astype(F32), other_refs[chain][place, rows, :].astype(F32))
    gen = -fock_ref[...] / hess_ref[...]
    square = jnp.sum(jnp.sum(gen * gen, axis=0, keepdims=True), axis=1, keepdims=True)
    rot = gen * jnp.minimum(1.0, math.sqrt(n_occ) / jnp.sqrt(square))
    rot_b = rot.astype(BF16)
    rot_ref[...] = rot_b
    over = matmul(rot_b, rot_b, NT)
    over_b = over.astype(BF16)
    over2 = matmul(over_b, over_b, NN)
    over_rot = matmul(over_b, rot_b, NN)
    eye = jnp.where(
        lax.broadcasted_iota(jnp.int32, (n_occ, n_occ), 0) == lax.broadcasted_iota(jnp.int32, (n_occ, n_occ), 1),
        1.0, 0.0)
    u_oo = (eye - over / 2.0 + over2 / 24.0).astype(BF16)
    u_ref[:, :base] = u_oo[:, :base]
    u_ref[:, base:] = (rot - over_rot / 6.0).astype(BF16)
    u_ref[:, base:n_occ] = u_oo[:, base:]
    chosen = matmul(sel_ref[...], u_ref[...], NN)
    chosen_ref[...] = chosen.T[:n_mo].astype(BF16)
    q_loc, r_loc, n_mo = three_ref.shape
    rem = r_loc - main
    n_dev, dest_rows = sent_ref.shape[:2]
    for q in range(q_loc):
        product = matmul(three_ref[q], chosen_ref[...], NN)
        half_ref[q] = product[:main].T
        rem_ref[q * rem : (q + 1) * rem, :] = product[main:]
    l_oo = (over / 6.0 - eye).astype(BF16)
    left_ref[:, :base] = l_oo[:, :base]
    left_ref[:, base:] = (over_rot / 24.0 - rot / 2.0).astype(BF16)
    left_ref[:, base:n_occ] = l_oo[:, base:]
    turned = rem_ref[...].T

    def group(at, dest):
        tile, k = divmod(at, n_rows)
        if tile < main // LANES:
            rows = slice(k * n_dev + dest, k * n_dev + dest + 8)
            return swap_rows([half_ref[q, rows, tile * LANES : (tile + 1) * LANES] for q in range(q_loc)])
        zero = jnp.zeros((8, LANES), F32)
        if at > main // LANES * n_rows:
            return [zero] * 8
        rest = [turned[k * n_dev + dest : k * n_dev + dest + 8, :] for k in range(n_rows)]
        return swap_rows(rest + [zero] * (8 - n_rows))

    for dest in range(0, n_dev, 8):
        for at in range(0, dest_rows // 8, 2):
            for d, pair in enumerate(zip(group(at, dest), group(at + 1, dest))):
                sent_ref[dest + d, at * 8 : at * 8 + 16, :] = jnp.concatenate(pair, 0).astype(BF16)


def owner_kernel(n_rows, n_aux, q_loc, r_loc, main, got_ref, left_ref, rot_ref, out_ref):
    n_orb = got_ref.shape[1]
    places = pl.ds(pl.program_id(0) * n_aux, n_aux)
    n_occ, wide = left_ref.shape
    width = rot_ref.shape[1]
    base = wide - width
    n_mo = n_orb * r_loc
    n_vir = n_mo - n_occ
    rem = r_loc - main
    group = n_rows * q_loc
    rows = n_aux * group
    lane_q = lax.broadcasted_iota(jnp.int32, (n_aux, q_loc, LANES), 2) // rem
    own_q = lane_q == lax.broadcasted_iota(jnp.int32, (n_aux, q_loc, LANES), 1)
    e_row = lax.broadcasted_iota(jnp.int32, (LANES, LANES), 0) % rem
    e_col = lax.broadcasted_iota(jnp.int32, (LANES, LANES), 1)

    sources = []
    rest = jnp.zeros((rows, LANES), F32)
    for b in range(n_orb):
        block = got_ref[places, b, :, :].astype(F32)
        pieces = [block[:, c * group : (c + 1) * group, :].reshape(rows, LANES) for c in range(main // LANES)]
        last = main // LANES * group
        spread = [
            jnp.where(own_q, jnp.broadcast_to(block[:, last + k : last + k + 1, :], own_q.shape), 0.0)
            for k in range(n_rows)
        ]
        spread = jnp.concatenate(spread, 1).reshape(rows, LANES).astype(BF16)
        rest = rest + matmul(spread, jnp.where(e_row + b * rem == e_col, 1.0, 0.0).astype(BF16), NN)
        sources.append((lambda tile, pieces=pieces: pieces[tile], 0, b * r_loc, main))
    for b in range(n_orb):
        sources.append((lambda tile: rest, b * rem, b * r_loc + main, rem))
    sources.sort(key=lambda entry: entry[2])
    half = jnp.concatenate(assemble(sources, wide, rows), 1)
    inner = matmul(half.astype(BF16), left_ref[...], NT).astype(BF16)
    total = half[:, base:] + matmul(inner, rot_ref[...], NN)
    total = total.reshape(n_aux, group, width)
    per_row = [total[:, k * q_loc : (k + 1) * q_loc, :].reshape(n_aux * q_loc, width) for k in range(n_rows)]
    sources = [
        (lambda tile, value=value: value[:, tile * LANES : (tile + 1) * LANES], n_occ - base, k * n_vir, n_vir)
        for k, value in enumerate(per_row)
    ]
    length = n_rows * n_vir
    for at, value in enumerate(assemble(sources, length, n_aux * q_loc)):
        stop = min(length, (at + 1) * LANES)
        out_ref[:, at * LANES : stop] = value[:, : stop - at * LANES].astype(BF16)


def on_device(n_aux, n_orb, three_index, density, hess_diag):
    n_dev = n_aux * n_orb
    q_loc, r_loc, n_mo = three_index.shape
    n_occ = density.shape[2]
    n_vir = n_mo - n_occ
    occ_blk = n_occ // n_orb
    pairs = occ_blk * n_vir // n_aux
    base = n_occ // LANES * LANES
    tiles = -(-(n_mo - base) // LANES)
    width = tiles * LANES
    main = r_loc // LANES * LANES
    assert n_dev & (n_dev - 1) == 0 and n_dev >= 8 and tiles % 4 == 0
    tracks = tracks_of(n_dev)
    whole = lambda *shape: pl.BlockSpec(shape, lambda *_: (0,) * len(shape))
    in_vmem = pl.BlockSpec(memory_space=pltpu.VMEM)

    chains = 2
    half_shape = (2, tiles * n_occ // (4 * chains), LANES)
    in_hbm = pl.BlockSpec(memory_space=pltpu.HBM)
    *parts, three_vmem = pl.pallas_call(
        functools.partial(fock_kernel, n_orb, n_dev, tracks),
        in_specs=[in_hbm, in_hbm],
        out_specs=[in_vmem] * (2 * chains + 1),
        out_shape=[
            *[jax.ShapeDtypeStruct(half_shape, F32)] * chains,
            *[jax.ShapeDtypeStruct(half_shape, BF16)] * chains,
            jax.ShapeDtypeStruct(three_index.shape, BF16),
        ],
        scratch_shapes=[
            pltpu.VMEM((tiles * n_occ, LANES), F32),
            pltpu.VMEM((q_loc, n_occ, r_loc), BF16),
            pltpu.SemaphoreType.DMA((q_loc,)),
            pltpu.SemaphoreType.DMA((q_loc,)),
        ],
        compiler_params=pltpu.CompilerParams(vmem_limit_bytes=38 * MIB),
        cost_estimate=pl.CostEstimate(
            flops=2 * q_loc * r_loc * n_occ * n_mo, bytes_accessed=2 * q_loc * r_loc * n_mo, transcendentals=0),
        name="fock",
    )(to_hbm(three_index), to_hbm(density.transpose(0, 2, 1)))
    hess = jnp.pad(
        hess_diag.T, ((0, 0), (n_occ - base, width - (n_mo - base))), constant_values=jnp.inf)

    masks = [[1 | 1 << tracks[half_of(d, n_dev)][k] for d in range(n_dev)] for k in range(len(tracks[0]))]
    held, other = [], []
    for chain in range(chains):
        part = parts[chain] + swap(parts[chains + chain], [1] * n_dev).astype(F32)
        piece = part[0] + swap(part[1].astype(BF16), masks[0]).astype(F32)
        for mask in masks[1:]:
            piece = piece + swap(piece.astype(BF16), mask).astype(F32)
        piece = piece.astype(BF16)
        held.append(jnp.stack([piece, swap(piece, masks[0])]))
        other.append(swap(held[chain], [1] * n_dev))

    assert q_loc == 8
    first = [p * pairs // n_vir for p in range(n_aux)]
    n_rows = max(-(-(p + 1) * pairs // n_vir) - first[p] for p in range(n_aux))
    sel = np.zeros((n_rows, n_aux, n_orb, n_occ), np.float32)
    for k in range(n_rows):
        for p in range(n_aux):
            for b in range(n_orb):
                sel[k, p, b, b * occ_blk + min(first[p] + k, occ_blk - 1)] = 1.0
    sel = jnp.asarray(sel.reshape(n_rows * n_dev, n_occ), BF16)

    dest_rows = -(-(main // LANES * n_rows * q_loc + n_rows) // 16) * 16
    wide = base + width
    sent, left, rot = pl.pallas_call(
        functools.partial(rotate_kernel, n_orb, n_dev, tracks, n_rows, main),
        in_specs=[in_vmem] * (2 * chains + 3),
        out_specs=[in_vmem] * 3,
        out_shape=[
            jax.ShapeDtypeStruct((n_dev, dest_rows, LANES), BF16),
            jax.ShapeDtypeStruct((n_occ, wide), BF16),
            jax.ShapeDtypeStruct((n_occ, width), BF16),
        ],
        scratch_shapes=[
            pltpu.VMEM((n_occ, width), F32),
            pltpu.VMEM((n_occ, wide), BF16),
            pltpu.VMEM((n_mo, n_rows * n_dev), BF16),
            pltpu.VMEM((q_loc * (r_loc - main), n_rows * n_dev), F32),
            pltpu.VMEM((q_loc, n_rows * n_dev, main), F32),
        ],
        compiler_params=pltpu.CompilerParams(vmem_limit_bytes=40 * MIB),
        cost_estimate=pl.CostEstimate(
            flops=2 * q_loc * r_loc * n_rows * n_dev * n_mo, bytes_accessed=2 * q_loc * r_loc * n_mo, transcendentals=0),
        name="half_rotation",
    )(*held, *other, hess, sel, three_vmem)

    got = lax.all_to_all(sent, BOTH, 0, 0, tiled=True).reshape(n_aux, n_orb, dest_rows, LANES)
    aux_step = min(n_aux, 8)
    out = pl.pallas_call(
        functools.partial(owner_kernel, n_rows, aux_step, q_loc, r_loc, main),
        grid=(n_aux // aux_step,),
        in_specs=[in_vmem] * 3,
        out_specs=pl.BlockSpec((aux_step * q_loc, n_rows * n_vir), lambda g: (g, 0)),
        out_shape=jax.ShapeDtypeStruct((n_aux * q_loc, n_rows * n_vir), BF16),
        compiler_params=pltpu.CompilerParams(vmem_limit_bytes=40 * MIB),
        cost_estimate=pl.CostEstimate(
            flops=4 * n_aux * q_loc * n_rows * n_occ * n_mo, bytes_accessed=8 * MIB, transcendentals=0),
        name="owner_rows",
    )(got, left, rot)
    if n_rows * n_vir != pairs:
        start = (lax.axis_index("aux") * pairs) % n_vir
        out = lax.dynamic_slice_in_dim(out, start, pairs, 1)
    return out[None]


def solution(mesh):
    def body(*args):
        return on_device(mesh.shape["aux"], mesh.shape["orb"], *args)

    return jax.shard_map(
        body,
        mesh=mesh,
        in_specs=(P("aux", "orb", None), P("aux", "orb", None), P()),
        out_specs=P("orb", None, "aux"),
        check_vma=False,
    )
```
